256 devices in a mesh: frame: 16 (over z_lo, y, core), tensor: 16 (over z_hi, x).
Axes of the slice: x: 4, y: 4, z: 8 (z_hi: 4, z_lo: 2; z = z_hi * 2 + z_lo), core: 2. Of those that a mesh axis runs over, the one named last changes fastest.
Arguments:
- latent: bfloat16 [30720, 1152], P('frame', 'tensor'), may hold values from -6 to 6
- timestep: int32 [1], replicated, may hold values from 0 to 999
- frame_pos: int32 [16], P('frame'), may hold values from 0 to 4095
- time_w1: bfloat16 [256, 1152], replicated, may hold values from -0.375 to 0.375
- time_w2: bfloat16 [1152, 1152], P(None, 'tensor'), may hold values from -0.1875 to 0.1875
- ada_w: bfloat16 [1152, 10368], P('tensor'), may hold values from -0.1875 to 0.1875
- w_sqkv: bfloat16 [1152, 3456], P(None, 'tensor'), may hold values from -0.70710678 to 0.70710678
- w_so: bfloat16 [1152, 1152], P('tensor'), may hold values from -0.25 to 0.25
- w_tqkv: bfloat16 [1152, 3456], P(None, 'tensor'), may hold values from -0.70710678 to 0.70710678
- w_to: bfloat16 [1152, 1152], P('tensor'), may hold values from -0.25 to 0.25
- w_fc1: bfloat16 [1152, 4608], P(None, 'tensor'), may hold values from -0.1875 to 0.1875
- w_fc2: bfloat16 [4608, 1152], P('tensor'), may hold values from -0.125 to 0.125
Outputs:
- block_out: bfloat16 [30720, 1152], P('frame', 'tensor')
The draws below stay inside these ranges and needn't reach their ends.
All inputs are finite; a program needn't handle non-finite values.
Results may differ from the reference program's by a relative error of at most 0.025.
Values may be sent and summed in bfloat16 or wider, within the bound.
No kernel may reach another device: no remote copies, remote signals or barrier semaphores. Data moves between devices by JAX's collectives and lax.ppermute only.
A program may use at most 128 MiB of HBM per device.

```python
import math
import jax
import jax.numpy as jnp
from jax import lax

D = 1152
H = 16
FF = 4608
TEMB = 256
HD = 72
P_SIZE = 1920
F = 16
TOKENS = 30720
N_TENSOR = 16


def column_gains(key, strong, middle):
    order = jax.random.permutation(key, H)
    gains = jnp.where(order < 2, strong, jnp.where(order < 4, middle, 1.0)).astype(jnp.float32)
    query_or_key = jnp.arange(3 * HD) // HD < 2
    table = jnp.where(query_or_key[None, :], gains[:, None], jnp.float32(1.0))
    return table.reshape(3 * D)


def draw_w_sqkv(key, part):
    key = jax.random.fold_in(key, 11)
    gain_key, value_key = jax.random.split(key)
    base = jax.random.truncated_normal(value_key, -4.0, 4.0, (D, 3 * D), jnp.float32)
    gains = column_gains(gain_key, 5.0, 3.0)
    return (base * gains[None, :] * D ** (-0.5)).astype(jnp.bfloat16)


def draw_w_tqkv(key, part):
    key = jax.random.fold_in(key, 23)
    gain_key, value_key = jax.random.split(key)
    base = jax.random.truncated_normal(value_key, -4.0, 4.0, (D, 3 * D), jnp.float32)
    gains = column_gains(gain_key, 5.0, 3.0)
    return (base * gains[None, :] * D ** (-0.5)).astype(jnp.bfloat16)


def plant(result, stream_key, smallest, high):
    extent = result.shape
    place = [jax.random.randint(jax.random.fold_in(stream_key, axis), (), 0, extent[axis]) for axis in range(len(extent))]
    result = result.at[tuple(place)].set(smallest)
    longest = extent.index(max(extent))
    place[longest] = (place[longest] + 1) % extent[longest]
    return result.at[tuple(place)].set(high)


def with_spikes(values, own_key, source, target, parts, factor):
    owner, partner = [(jnp.arange(values.shape[position]) // (values.shape[position] // parts)).reshape([-1 if axis == position else 1 for axis in range(values.ndim)]) for position in (source, target)]
    chosen = jax.random.permutation(own_key, parts)[partner]
    strong = (owner == chosen) | (owner == (partner + parts // 2) % parts)
    return jnp.where(strong, factor * values, values)


def shard_levels(stream_key, dims, cuts, low, largest):
    def one(position, blocks):
        heights = jax.random.uniform(jax.random.fold_in(jax.random.fold_in(stream_key, 6), position), (blocks,), jnp.float32, low / len(cuts), largest / len(cuts))
        return jnp.repeat(jnp.exp(heights), dims[position] // blocks).reshape((-1,) + (1,) * (len(dims) - position - 1))

    loudness = one(*cuts[0])
    for cut in cuts[1:]:
        loudness = loudness * one(*cut)
    return loudness


def scatter_about(key, extent, scale, limit, shards=(), kind=jnp.bfloat16):
    loudness = shard_levels(key, extent, shards, -0.22, 0.18) if shards else 1.0
    values = jax.random.normal(key, extent, jnp.float32) * scale * loudness
    return jnp.minimum(jnp.maximum(values, -limit), limit).astype(kind)


def heavy_noise(own_key, shape, scale, limit, shards, heavy, held_as=jnp.bfloat16):
    entries = scale * jax.random.normal(own_key, shape, jnp.float32)
    if shards:
        entries = entries * shard_levels(own_key, shape, shards, -0.22, 0.18)
    return jnp.clip(with_spikes(entries, jax.random.fold_in(own_key, 3), *heavy), -limit, limit).astype(held_as)


def setup_inputs(seed: int = 0) -> dict:
    keys = jax.random.split(jax.random.key(seed), 13)
    latent = scatter_about(keys[0], (TOKENS, D), 1.0, 6.0, ((0, 16), (1, 16)))
    timestep = jax.random.randint(keys[1], (1,), 0, 1000).astype(jnp.int32)
    frame_pos = plant(jax.random.randint(keys[2], (F,), 0, 4096), jax.random.fold_in(keys[2], 1), 0, 4095).astype(jnp.int32)
    time_w1 = scatter_about(keys[3], (TEMB, D), TEMB ** -0.5, 0.375)
    time_w2 = scatter_about(keys[4], (D, D), D ** -0.5, 0.1875, ((1, 16),))
    ada_w = scatter_about(keys[5], (D, 9 * D), D ** -0.5, 0.1875, ((0, 16),))
    w_sqkv = draw_w_sqkv(jax.random.fold_in(keys[12], 71), 0)
    w_so = heavy_noise(keys[7], (D, D), D ** -0.5, 0.25, ((0, 16),), (0, 1, 16, 2.0))
    w_tqkv = draw_w_tqkv(jax.random.fold_in(keys[12], 71), 0)
    w_to = heavy_noise(keys[9], (D, D), D ** -0.5, 0.25, ((0, 16),), (0, 1, 16, 2.0))
    w_fc1 = scatter_about(keys[10], (D, FF), D ** -0.5, 0.1875, ((1, 16),))
    w_fc2 = heavy_noise(keys[11], (FF, D), FF ** -0.5, 0.125, ((0, 16),), (0, 1, 16, 2.0))
    return dict(latent=latent, timestep=timestep, frame_pos=frame_pos, time_w1=time_w1, time_w2=time_w2, ada_w=ada_w, w_sqkv=w_sqkv, w_so=w_so, w_tqkv=w_tqkv, w_to=w_to, w_fc1=w_fc1, w_fc2=w_fc2)


def layer_norm(values_in):
    center = values_in - lax.optimization_barrier(jnp.mean(values_in, axis=-1, keepdims=True))
    spread = lax.optimization_barrier(jnp.mean(center * center, axis=-1, keepdims=True))
    return center * lax.rsqrt(spread + 1e-06)

def branch_input(stream, shift, scale):
    return (layer_norm(stream.astype(jnp.float32)) * (1.0 + scale) + shift).astype(jnp.bfloat16)

def time_features(timestep, width):
    half_width = width // 2
    frequency = jnp.exp(-math.log(10000.0) * jnp.arange(half_width, dtype=jnp.float32) / half_width)
    angles = timestep.astype(jnp.float32)[:, None] * frequency[None, :]
    return jnp.concatenate([jnp.cos(angles), jnp.sin(angles)], axis=1).astype(jnp.bfloat16)

def rotate(projected, positions):
    half_width = HD // 2
    frequency = jnp.exp(-math.log(10000.0) * jnp.arange(half_width, dtype=jnp.float32) / half_width)
    angles = positions.astype(jnp.float32)[:, None] * frequency[None, :]
    cosine = jnp.cos(angles)[:, None, None, :]
    sine_part = jnp.sin(angles)[:, None, None, :]

    def turn(section):
        section = section.astype(jnp.float32)
        first_half = section[..., :half_width]
        second_half = section[..., half_width:]
        turned = jnp.concatenate([first_half * cosine - second_half * sine_part, first_half * sine_part + second_half * cosine], axis=-1)
        return turned.astype(jnp.bfloat16)
    return (turn(projected[:, :, :, 0]), turn(projected[:, :, :, 1]), projected[:, :, :, 2])

def grouped(activation, weight):
    group_width = activation.shape[1] // N_TENSOR

    def add_group(index, total):
        start = index * group_width
        columns = lax.dynamic_slice_in_dim(activation, start, group_width, 1)
        rows_part = lax.dynamic_slice_in_dim(weight, start, group_width, 0)
        term = jnp.dot(columns, rows_part, preferred_element_type=jnp.float32).astype(jnp.bfloat16)
        term = lax.optimization_barrier(term)
        return total + term.astype(jnp.float32)
    empty = jnp.zeros((activation.shape[0], weight.shape[1]), jnp.float32)
    return lax.fori_loop(0, N_TENSOR, add_group, empty)

def reference(latent, timestep, frame_pos, time_w1, time_w2, ada_w, w_sqkv, w_so, w_tqkv, w_to, w_fc1, w_fc2):
    time_embed = time_features(timestep, TEMB)
    hidden_time = jax.nn.silu(jnp.dot(time_embed, time_w1, preferred_element_type=jnp.float32)).astype(jnp.bfloat16)
    condition = jax.nn.silu(jnp.dot(hidden_time, time_w2, preferred_element_type=jnp.float32)).astype(jnp.bfloat16)
    modulation = jnp.dot(condition, ada_w, preferred_element_type=jnp.float32)[0]

    def mod_vector(index):
        return modulation[index * D:(index + 1) * D]
    scale_factor = HD ** (-0.5)
    normed = branch_input(latent, mod_vector(0), mod_vector(1))
    projected = jnp.dot(normed, w_sqkv, preferred_element_type=jnp.float32).astype(jnp.bfloat16)
    projected = projected.reshape(F, P_SIZE, H, 3, HD)

    def frame_attention(frame_qkv):
        queries = frame_qkv[:, :, 0].astype(jnp.float32)
        keys_all = frame_qkv[:, :, 1].astype(jnp.float32)
        values_all = frame_qkv[:, :, 2].astype(jnp.float32)
        scores = jnp.einsum('phd,qhd->hpq', queries, keys_all) * scale_factor
        weights = jax.nn.softmax(scores, axis=-1).astype(jnp.bfloat16)
        return jnp.einsum('hpq,qhd->phd', weights.astype(jnp.float32), values_all).astype(jnp.bfloat16)
    attended = lax.map(frame_attention, projected).reshape(TOKENS, D)
    stream = (latent.astype(jnp.float32) + mod_vector(2) * grouped(attended, w_so)).astype(jnp.bfloat16)
    normed = branch_input(stream, mod_vector(3), mod_vector(4))
    projected = jnp.dot(normed, w_tqkv, preferred_element_type=jnp.float32).astype(jnp.bfloat16)
    projected = projected.reshape(F, P_SIZE, H, 3, HD)
    queries, keys_all, values_all = rotate(projected, frame_pos)
    scores = jnp.einsum('fphd,gphd->phfg', queries.astype(jnp.float32), keys_all.astype(jnp.float32)) * scale_factor
    weights = jax.nn.softmax(scores, axis=-1).astype(jnp.bfloat16)
    attended = jnp.einsum('phfg,gphd->fphd', weights.astype(jnp.float32), values_all.astype(jnp.float32)).astype(jnp.bfloat16)
    attended = attended.reshape(TOKENS, D)
    stream = (stream.astype(jnp.float32) + mod_vector(5) * grouped(attended, w_to)).astype(jnp.bfloat16)
    normed = branch_input(stream, mod_vector(6), mod_vector(7))
    mlp_hidden = jax.nn.gelu(jnp.dot(normed, w_fc1, preferred_element_type=jnp.float32), approximate=True).astype(jnp.bfloat16)
    return (stream.astype(jnp.float32) + mod_vector(8) * grouped(mlp_hidden, w_fc2)).astype(jnp.bfloat16)
```

```python
import math

import jax
import jax.numpy as jnp
from jax import lax
from jax.experimental import pallas as pl
from jax.experimental.pallas import tpu as pltpu
from jax.sharding import PartitionSpec as P

D = 1152
HD = 72
P_SIZE = 1920
N_T = 16
ROWS = P_SIZE // N_T
FF_PART = 36
SCALE_LOG2 = HD ** (-0.5) * math.log2(math.e)
Q_BLOCK = 384
F32 = jnp.float32
BF16 = jnp.bfloat16


def layer_norm(values_in):
    center = values_in - jnp.mean(values_in, axis=-1, keepdims=True)
    spread = jnp.mean(center * center, axis=-1, keepdims=True)
    return center * lax.rsqrt(spread + 1e-06)


def branch_input(stream, shift, scale):
    return (layer_norm(stream.astype(F32)) * (1.0 + scale) + shift).astype(BF16)


def time_features(timestep, width):
    half_width = width // 2
    frequency = jnp.exp(-math.log(10000.0) * jnp.arange(half_width, dtype=F32) / half_width)
    angles = timestep.astype(F32)[:, None] * frequency[None, :]
    return jnp.concatenate([jnp.cos(angles), jnp.sin(angles)], axis=1).astype(BF16)


def dot(a, b, contract=((1,), (0,))):
    return lax.dot_general(a, b, (contract, ((), ())), preferred_element_type=F32)


def move_frame(v, dzl=0, dy=0, dcore=0):
    pairs = []
    for source in range(16):
        zl, y, core = source // 8, source // 2 % 4, source % 2
        pairs.append((source, (zl ^ dzl) * 8 + (y + dy) % 4 * 2 + (core ^ dcore)))
    return lax.ppermute(v, "frame", pairs)


def gather_rows(own):
    half = 64
    before = move_frame(own, dy=1)
    after = move_frame(own, dy=-1)
    far_a = move_frame(before[:half], dy=1)
    far_b = move_frame(after[half:], dy=-1)
    column = jnp.concatenate([own, after, far_a, far_b, before], axis=0)
    return jnp.concatenate([column, move_frame(column, dcore=1)], axis=0)


def scatter_rows(partial):
    half = 64
    n = partial.shape[0] // 2
    partial = partial.astype(BF16)
    column = partial[:n].astype(F32) + move_frame(partial[n:], dcore=1).astype(F32)
    blocks = column.reshape(4, n // 4, partial.shape[1])
    far = blocks[2].astype(BF16)
    got_a = move_frame(far[:half], dy=1).astype(F32)
    got_b = move_frame(far[half:], dy=-1).astype(F32)
    up = jnp.concatenate([blocks[1][:half] + got_a, blocks[1][half:]], axis=0).astype(BF16)
    down = jnp.concatenate([blocks[3][:half], blocks[3][half:] + got_b], axis=0).astype(BF16)
    return blocks[0] + move_frame(up, dy=1).astype(F32) + move_frame(down, dy=-1).astype(F32)


def spatial_kernel(qkv_ref, out_ref, keys, values):
    @pl.when(pl.program_id(0) == 0)
    def _():
        keys[...] = qkv_ref[HD : 2 * HD, :].astype(F32).T.astype(BF16)
        values[:HD, :] = qkv_ref[2 * HD :, :].astype(F32)
        values[HD:, :] = jnp.ones((8, P_SIZE), F32)

    start = pl.multiple_of(pl.program_id(0) * Q_BLOCK, 128)
    queries = qkv_ref[:HD, pl.ds(start, Q_BLOCK)]
    scores = dot(keys[...], queries)
    top = jnp.max(scores, axis=0, keepdims=True)
    weights = jnp.exp2((scores - top) * SCALE_LOG2).astype(BF16)
    summed = dot(values[...].astype(BF16), weights)
    out_ref[...] = (summed[:HD] / summed[HD : HD + 1]).astype(BF16)


def spatial_attention(qkv):
    return pl.pallas_call(
        spatial_kernel,
        grid=(P_SIZE // Q_BLOCK,),
        out_shape=jax.ShapeDtypeStruct((HD, P_SIZE), BF16),
        in_specs=[pl.BlockSpec((3 * HD, P_SIZE), lambda i: (0, 0))],
        out_specs=pl.BlockSpec((HD, Q_BLOCK), lambda i: (0, i)),
        scratch_shapes=[pltpu.VMEM((P_SIZE, HD), BF16), pltpu.VMEM((HD + 8, P_SIZE), F32)],
        compiler_params=pltpu.CompilerParams(vmem_limit_bytes=32 * 2**20),
        cost_estimate=pl.CostEstimate(
            flops=4 * P_SIZE * P_SIZE * HD, bytes_accessed=4 * HD * P_SIZE * 2, transcendentals=P_SIZE * P_SIZE
        ),
    )(qkv)


def temporal_kernel(own_ref, other_ref, swap_ref, cos_ref, sin_ref, out_own_ref, out_other_ref, rotated, result):
    for index, ref in ((0, own_ref), (1, other_ref)):
        block = ref[...]
        swapped = dot(block, swap_ref[...]).reshape(8, ROWS, 3 * HD)
        rows = pl.ds(8 * index, 8)
        rotated[rows] = (
            block.astype(F32).reshape(8, ROWS, 3 * HD) * cos_ref[rows] + swapped * sin_ref[rows]
        )
    row = lax.broadcasted_iota(jnp.int32, (128, 128), 0)
    column = lax.broadcasted_iota(jnp.int32, (128, 128), 1)
    same = (row % 8) == (column % 8)
    for group in range(ROWS // 8):
        section = rotated[:, 8 * group : 8 * group + 8, :].reshape(128, 3 * HD).astype(BF16)
        queries, keys, values = section[:, :HD], section[:, HD : 2 * HD], section[:, 2 * HD :]
        scores = jnp.where(same, dot(queries, keys, ((1,), (1,))), -jnp.inf)
        top = jnp.max(scores, axis=1, keepdims=True)
        weights = jnp.exp2((scores - top) * SCALE_LOG2)
        weights = (weights / jnp.sum(weights, axis=1, keepdims=True)).astype(BF16)
        result[:, 8 * group : 8 * group + 8, :] = dot(weights, values).reshape(16, 8, HD)
    out_own_ref[...] = result[:8].reshape(8 * ROWS, HD).astype(BF16)
    out_other_ref[...] = result[8:].reshape(8 * ROWS, HD).astype(BF16)


def temporal_attention(own, other, cosine, sine):
    lane = jnp.arange(3 * HD)
    half = HD // 2
    partner = jnp.where(lane % HD < half, lane + half, lane - half)
    swap = ((lane[:, None] == partner[None, :]) & (lane[None, :] < 2 * HD)).astype(BF16)
    shape = jax.ShapeDtypeStruct((8 * ROWS, HD), BF16)
    return pl.pallas_call(
        temporal_kernel,
        out_shape=(shape, shape),
        scratch_shapes=[pltpu.VMEM((16, ROWS, 3 * HD), F32), pltpu.VMEM((16, ROWS, HD), F32)],
        compiler_params=pltpu.CompilerParams(vmem_limit_bytes=32 * 2**20),
        cost_estimate=pl.CostEstimate(
            flops=16 * ROWS * 128 * HD * 4, bytes_accessed=16 * ROWS * HD * 8, transcendentals=16 * ROWS * 128
        ),
    )(own, other, swap, cosine, sine)


def shards(
    latent, timestep, frame_pos, time_w1, time_w2, ada_w, w_sqkv, w_so, w_tqkv, w_to, w_fc1, w_fc2
):
    frame = lax.axis_index("frame")
    tensor = lax.axis_index("tensor")
    zl, y, core = frame // 8, frame // 2 % 4, frame % 2

    full_rows = lax.all_gather(latent, "tensor", axis=1, tiled=True)
    so_half = lax.all_gather(
        lax.dynamic_slice_in_dim(w_so, core * (D // 2), D // 2, 1), "tensor", axis=0, tiled=True
    )
    part = (y * 2 + core) * FF_PART
    fc_own = jnp.concatenate(
        [
            lax.dynamic_slice_in_dim(w_fc1, part, FF_PART, 1).T,
            lax.dynamic_slice_in_dim(w_fc2, part, FF_PART, 0),
        ],
        axis=0,
    )
    fc_all = lax.all_gather(fc_own, "tensor", axis=0, tiled=True).reshape(N_T, 2, FF_PART, D)
    pairs = []
    for f in range(16):
        head = f // 2 % 4 * 4 + f % 2 * 2 + f // 8
        pairs.extend((t * 16 + head, f * 16 + t) for t in range(16))
    head_w = jnp.concatenate([w_tqkv.T, w_to], axis=0)
    head_a = lax.ppermute(head_w, ("frame", "tensor"), pairs)
    head_b = move_frame(head_a, dzl=1)

    time_embed = time_features(timestep, time_w1.shape[0])
    hidden_time = jax.nn.silu(dot(time_embed, time_w1)).astype(BF16)
    condition = jax.nn.silu(dot(hidden_time, time_w2)).astype(BF16)
    mod_terms = dot(condition, ada_w).astype(BF16).reshape(1, 81, 128)
    mod_terms = lax.all_to_all(jnp.broadcast_to(mod_terms, (N_T, 81, 128)), "tensor", 0, 0)
    modulation = jnp.sum(mod_terms.astype(F32), axis=0).reshape(9, D)

    positions = lax.all_to_all(jnp.broadcast_to(frame_pos[None], (16, 1)), "frame", 0, 0)[:, 0]
    slot = jnp.arange(16)
    order = ((slot // 8) ^ zl) * 8 + (y + slot % 4) % 4 * 2 + ((slot // 4 % 2) ^ core)
    positions = jnp.take(positions, order).astype(F32)
    half = HD // 2
    frequency = jnp.exp(-math.log(10000.0) * jnp.arange(half, dtype=F32) / half)
    angles = positions[:, None] * frequency[None, :]
    cosine, sine = jnp.cos(angles), jnp.sin(angles)
    one, zero = jnp.ones((16, HD), F32), jnp.zeros((16, HD), F32)
    cosine = jnp.concatenate([cosine] * 4 + [one], axis=1)[:, None, :]
    sine = jnp.concatenate([-sine, sine] * 2 + [zero], axis=1)[:, None, :]

    normed = branch_input(full_rows, modulation[0], modulation[1])
    qkv = dot(w_sqkv, normed, ((0,), (1,))).astype(BF16)
    attended = spatial_attention(qkv)
    attended = lax.all_to_all(attended, "tensor", split_axis=1, concat_axis=0, tiled=True)
    attended = jnp.concatenate([attended, move_frame(attended, dcore=1)], axis=1)
    mine = dot(attended, so_half, ((0,), (0,))).astype(BF16)
    theirs = move_frame(mine[ROWS:], dcore=1)
    mine = mine[:ROWS]
    projected = jnp.where(
        core == 0, jnp.concatenate([mine, theirs], axis=1), jnp.concatenate([theirs, mine], axis=1)
    ).astype(F32)
    stream = lax.dynamic_slice_in_dim(full_rows, tensor * ROWS, ROWS, 0)
    stream = (stream.astype(F32) + modulation[2] * projected).astype(BF16)

    rows = gather_rows(branch_input(stream, modulation[3], modulation[4]))
    qkv_b = dot(rows, head_b[: 3 * HD], ((1,), (1,))).astype(BF16)
    qkv_b = move_frame(qkv_b, dzl=1)
    qkv_a = dot(rows, head_a[: 3 * HD], ((1,), (1,))).astype(BF16)
    out_a, out_b = temporal_attention(qkv_a, qkv_b, cosine, sine)
    out_b = move_frame(out_b, dzl=1)
    partial = dot(out_a, head_a[3 * HD :]) + dot(out_b, head_b[3 * HD :])
    stream = (stream.astype(F32) + modulation[5] * scatter_rows(partial)).astype(BF16)

    rows = gather_rows(branch_input(stream, modulation[6], modulation[7]))
    fc1 = fc_all[:, 0].reshape(N_T * FF_PART, D)
    fc2 = fc_all[:, 1].reshape(N_T * FF_PART, D)
    hidden = jax.nn.gelu(dot(rows, fc1, ((1,), (1,))), approximate=True).astype(BF16)
    stream = stream.astype(F32) + modulation[8] * scatter_rows(dot(hidden, fc2))
    return lax.all_to_all(stream.astype(BF16), "tensor", split_axis=1, concat_axis=0, tiled=True)


def solution(mesh):
    placed = (
        P("frame", "tensor"),
        P(),
        P("frame"),
        P(),
        P(None, "tensor"),
        P("tensor", None),
        P(None, "tensor"),
        P("tensor", None),
        P(None, "tensor"),
        P("tensor", None),
        P(None, "tensor"),
        P("tensor", None),
    )
    return jax.shard_map(
        shards, mesh=mesh, in_specs=placed, out_specs=P("frame", "tensor"), check_vma=False
    )
```

```python
import math

import jax
import jax.numpy as jnp
from jax import lax
from jax.experimental import pallas as pl
from jax.experimental.layout import Layout, with_layout_constraint
from jax.experimental.pallas import tpu as pltpu
from jax.sharding import PartitionSpec as P

D = 1152
HD = 72
P_SIZE = 1920
N_T = 16
ROWS = P_SIZE // N_T
FF_PART = 72
SCALE_LOG2 = HD ** (-0.5) * math.log2(math.e)
Q_BLOCK = 384
PAD = 80
F32 = jnp.float32
BF16 = jnp.bfloat16


def layer_norm(values_in):
    center = values_in - jnp.mean(values_in, axis=-1, keepdims=True)
    spread = jnp.mean(center * center, axis=-1, keepdims=True)
    return center * lax.rsqrt(spread + 1e-06)


def branch_input(stream, shift, scale):
    return (layer_norm(stream.astype(F32)) * (1.0 + scale) + shift).astype(BF16)


def time_features(timestep, width):
    half_width = width // 2
    frequency = jnp.exp(-math.log(10000.0) * jnp.arange(half_width, dtype=F32) / half_width)
    angles = timestep.astype(F32)[:, None] * frequency[None, :]
    return jnp.concatenate([jnp.cos(angles), jnp.sin(angles)], axis=1).astype(BF16)


def dot(a, b, contract=((1,), (0,))):
    return lax.dot_general(a, b, (contract, ((), ())), preferred_element_type=F32)


def row_major(v):
    return with_layout_constraint(v, Layout(major_to_minor=tuple(range(v.ndim))))


def move_frame(v, dzl=0, dy=0, dcore=0):
    pairs = []
    for source in range(16):
        zl, y, core = source // 8, source // 2 % 4, source % 2
        pairs.append((source, (zl ^ dzl) * 8 + (y + dy) % 4 * 2 + (core ^ dcore)))
    return lax.ppermute(v, "frame", pairs)


def move_tensor(v, dzh=0, dx=0):
    pairs = []
    for source in range(16):
        zh, x = source // 4, source % 4
        pairs.append((source, (zh + dzh) % 4 * 4 + (x + dx) % 4))
    return lax.ppermute(v, "tensor", pairs)


def ring(own, move, half):
    return ring_far(own, move(own, 1), move(own, -1), move, half)


def ring_far(own, before, after, move, half):
    return own, after, move(before[:half], 1), move(after[half:], -1), before


def ring_in_halves(top, low, move):
    before_top, after_low = move(top, 1), move(low, -1)
    before_low, after_top = move(low, 1), move(top, -1)
    far_top, far_low = move(before_top, 1), move(after_low, -1)
    return (top, low), (after_top, after_low), (far_top, far_low), (before_top, before_low)


def placed_rows(blocks, rows, position):
    size = sum(part.shape[0] for part in blocks[0])
    out = jnp.zeros((4, rows[1] - rows[0]) + blocks[0][0].shape[1:], blocks[0][0].dtype)
    for step, parts in enumerate(blocks):
        start = 0
        for part in parts:
            stop = start + part.shape[0]
            low, high = max(start, rows[0]), min(stop, rows[1])
            if low < high:
                piece = part[low - start : high - start][None]
                out = lax.dynamic_update_slice(out, piece, ((position + step) % 4, low - rows[0], 0))
            start = stop
    return out.reshape((4 * (rows[1] - rows[0]),) + out.shape[2:])


def along_zh(v, d):
    return move_tensor(v, dzh=d)


def along_x(v, d):
    return move_tensor(v, dx=d)


def along_y(v, d):
    return move_frame(v, dy=d)


def gather_rows(own):
    column = row_major(jnp.concatenate(ring(row_major(own), along_y, 64), axis=0))
    return row_major(jnp.concatenate([column, move_frame(column, dcore=1)], axis=0))


def scatter_rows(partial):
    half = 64
    n = partial.shape[0] // 2
    partial = partial.astype(BF16)
    column = partial[:n].astype(F32) + move_frame(partial[n:], dcore=1).astype(F32)
    blocks = column.reshape(4, n // 4, partial.shape[1])
    far = blocks[2].astype(BF16)
    got_a = move_frame(far[:half], dy=1).astype(F32)
    got_b = move_frame(far[half:], dy=-1).astype(F32)
    up = jnp.concatenate([blocks[1][:half] + got_a, blocks[1][half:]], axis=0).astype(BF16)
    down = jnp.concatenate([blocks[3][:half], blocks[3][half:] + got_b], axis=0).astype(BF16)
    return blocks[0] + move_frame(up, dy=1).astype(F32) + move_frame(down, dy=-1).astype(F32)


def spatial_kernel(*refs):
    pieces, (weight_ref, shift_scale_ref, out_ref, queries, keys, values) = refs[:8], refs[8:]

    @pl.when(pl.program_id(0) == 0)
    def _():
        shift_scale = shift_scale_ref[...].T
        shift, scale = shift_scale[:, 0:1], 1.0 + shift_scale[:, 1:2]
        ones_row = lax.broadcasted_iota(jnp.int32, (PAD, Q_BLOCK), 0) == HD
        for part in range(P_SIZE // Q_BLOCK):
            columns = slice(part * Q_BLOCK, (part + 1) * Q_BLOCK)
            rows = [ref[:, columns] for ref in pieces]
            features = jnp.concatenate(rows, axis=0).astype(F32)
            center = features - jnp.mean(features, axis=0, keepdims=True)
            spread = jnp.mean(center * center, axis=0, keepdims=True)
            normed = center * lax.rsqrt(spread + 1e-06) * scale + shift
            qkv = dot(weight_ref[...], normed.astype(BF16))
            queries[:, columns] = qkv[:PAD].astype(BF16)
            keys[columns, :] = qkv[PAD : 2 * PAD].T.astype(BF16)
            values[:, columns] = jnp.where(ones_row, 1.0, qkv[2 * PAD :]).astype(BF16)

    start = pl.multiple_of(pl.program_id(0) * Q_BLOCK, 128)
    scores = dot(keys[...], queries[:, pl.ds(start, Q_BLOCK)])
    top = jnp.max(scores, axis=0, keepdims=True)
    weights = jnp.exp2((scores - top) * SCALE_LOG2).astype(BF16)
    summed = dot(values[...], weights)
    out_ref[...] = (summed[:HD] / summed[HD : HD + 1]).astype(BF16)


def spatial_attention(pieces, weight, shift_scale):
    whole = lambda v: pl.BlockSpec(v.shape, lambda i: (0, 0))
    operands = (*pieces, weight, shift_scale)
    return pl.pallas_call(
        spatial_kernel,
        grid=(P_SIZE // Q_BLOCK,),
        out_shape=jax.ShapeDtypeStruct((HD, P_SIZE), BF16),
        in_specs=[whole(v) for v in operands],
        out_specs=pl.BlockSpec((HD, Q_BLOCK), lambda i: (0, i)),
        scratch_shapes=[
            pltpu.VMEM((PAD, P_SIZE), BF16),
            pltpu.VMEM((P_SIZE, PAD), BF16),
            pltpu.VMEM((PAD, P_SIZE), BF16),
        ],
        compiler_params=pltpu.CompilerParams(vmem_limit_bytes=48 * 2**20),
        cost_estimate=pl.CostEstimate(
            flops=4 * P_SIZE * P_SIZE * HD + 2 * P_SIZE * D * 3 * HD,
            bytes_accessed=P_SIZE * D * 2,
            transcendentals=P_SIZE * P_SIZE,
        ),
    )(*operands)


def mlp_kernel(rows_ref, weight_ref, out_ref):
    total = jnp.zeros(out_ref.shape, F32)
    step = 384
    for start in range(0, D, step):
        units = slice(start, start + step)
        hidden = dot(rows_ref[...], weight_ref[units, :D], ((1,), (1,)))
        hidden = jax.nn.gelu(hidden, approximate=True).astype(BF16)
        total = total + dot(hidden, weight_ref[units, D:])
    out_ref[...] = total.astype(BF16)


def mlp(rows, weight):
    return pl.pallas_call(
        mlp_kernel,
        out_shape=jax.ShapeDtypeStruct(rows.shape, BF16),
        compiler_params=pltpu.CompilerParams(vmem_limit_bytes=40 * 2**20),
        cost_estimate=pl.CostEstimate(
            flops=4 * rows.shape[0] * D * D, bytes_accessed=6 * D * D, transcendentals=rows.shape[0] * D
        ),
    )(rows, weight)


def temporal_kernel(own_ref, other_ref, swap_ref, cos_ref, sin_ref, out_own_ref, out_other_ref, rotated, result):
    for index, ref in ((0, own_ref), (1, other_ref)):
        block = ref[...]
        swapped = dot(block, swap_ref[...]).reshape(8, ROWS, 3 * HD)
        rows = pl.ds(8 * index, 8)
        rotated[rows] = (
            block.astype(F32).reshape(8, ROWS, 3 * HD) * cos_ref[rows] + swapped * sin_ref[rows]
        )
    row = lax.broadcasted_iota(jnp.int32, (128, 128), 0)
    column = lax.broadcasted_iota(jnp.int32, (128, 128), 1)
    same = (row % 8) == (column % 8)
    for group in range(ROWS // 8):
        section = rotated[:, 8 * group : 8 * group + 8, :].reshape(128, 3 * HD).astype(BF16)
        queries, keys, values = section[:, :HD], section[:, HD : 2 * HD], section[:, 2 * HD :]
        scores = jnp.where(same, dot(queries, keys, ((1,), (1,))), -jnp.inf)
        top = jnp.max(scores, axis=1, keepdims=True)
        weights = jnp.exp2((scores - top) * SCALE_LOG2)
        weights = (weights / jnp.sum(weights, axis=1, keepdims=True)).astype(BF16)
        result[:, 8 * group : 8 * group + 8, :] = dot(weights, values).reshape(16, 8, HD)
    out_own_ref[...] = result[:8].reshape(8 * ROWS, HD).astype(BF16)
    out_other_ref[...] = result[8:].reshape(8 * ROWS, HD).astype(BF16)


def temporal_attention(own, other, cosine, sine):
    lane = jnp.arange(3 * HD)
    half = HD // 2
    partner = jnp.where(lane % HD < half, lane + half, lane - half)
    swap = ((lane[:, None] == partner[None, :]) & (lane[None, :] < 2 * HD)).astype(BF16)
    shape = jax.ShapeDtypeStruct((8 * ROWS, HD), BF16)
    return pl.pallas_call(
        temporal_kernel,
        out_shape=(shape, shape),
        scratch_shapes=[pltpu.VMEM((16, ROWS, 3 * HD), F32), pltpu.VMEM((16, ROWS, HD), F32)],
        compiler_params=pltpu.CompilerParams(vmem_limit_bytes=32 * 2**20),
        cost_estimate=pl.CostEstimate(
            flops=16 * ROWS * 128 * HD * 4, bytes_accessed=16 * ROWS * HD * 8, transcendentals=16 * ROWS * 128
        ),
    )(own, other, swap, cosine, sine)


def shards(
    latent, timestep, frame_pos, time_w1, time_w2, ada_w, w_sqkv, w_so, w_tqkv, w_to, w_fc1, w_fc2
):
    frame = lax.axis_index("frame")
    tensor = lax.axis_index("tensor")
    zl, y, core = frame // 8, frame // 2 % 4, frame % 2

    zh, x = tensor // 4, tensor % 4
    together = lax.optimization_barrier

    zh_groups = [[4 * i + j for i in range(4)] for j in range(4)]
    x_groups = [[4 * i + j for j in range(4)] for i in range(4)]

    own, after, far_top, far_low, before = ring(latent.T, along_zh, 40)
    blocks = (own,), (after,), (far_top, far_low), (before,)
    latent_top = placed_rows(blocks, (0, 40), zh)
    latent_low = placed_rows(blocks, (40, HD), zh)

    part = (zl * 2 + core) * FF_PART
    late = jnp.concatenate(
        [
            lax.dynamic_slice_in_dim(w_fc1, part, FF_PART, 1).T,
            lax.dynamic_slice_in_dim(w_fc2, part, FF_PART, 0),
            lax.dynamic_slice_in_dim(w_so, core * (D // 2), D // 2, 1),
        ],
        axis=1,
    )

    time_embed = time_features(timestep, time_w1.shape[0])
    hidden_time = jax.nn.silu(dot(time_embed, time_w1)).astype(BF16)
    condition = jax.nn.silu(dot(hidden_time, time_w2)).astype(BF16)
    width = 9 * D // 16
    terms = dot(condition, lax.dynamic_slice_in_dim(ada_w, frame * width, width, 1)).astype(BF16)
    terms = lax.all_to_all(jnp.broadcast_to(terms[None], (N_T, 1, width)), "tensor", 0, 0)
    latent_top, latent_low, terms, late = together((latent_top, latent_low, terms, late))
    late = lax.all_gather(late, "tensor", axis=0, tiled=True, axis_index_groups=zh_groups)
    blocks = ring_in_halves(latent_top, latent_low, along_x)
    summed = jnp.sum(terms.astype(F32), axis=0)
    packed = jnp.concatenate([summed, jnp.broadcast_to(frame_pos.astype(F32)[None], (1, 8))], axis=1)
    packed = lax.all_to_all(jnp.broadcast_to(packed[None], (16, 1, width + 8)), "frame", 0, 0)
    before, packed, w_tqkv, w_to = together((blocks[3], packed, w_tqkv, w_to))
    pieces = [part for block in (*blocks[:3], before) for part in block]
    stream = [[lax.dynamic_slice_in_dim(p, tensor * ROWS, ROWS, 1) for p in block] for block in blocks]
    stream_top = placed_rows([(block[0],) for block in stream], (0, 160), x)
    stream_low = placed_rows([(block[1],) for block in stream], (0, 128), x)
    modulation = packed[:, 0, :width].reshape(9, D)
    slot = jnp.arange(16)
    order = ((slot // 8) ^ zl) * 8 + (y + slot % 4) % 4 * 2 + ((slot // 4 % 2) ^ core)
    positions = jnp.take(packed[:, 0, width], order)
    half = HD // 2
    frequency = jnp.exp(-math.log(10000.0) * jnp.arange(half, dtype=F32) / half)
    angles = positions[:, None] * frequency[None, :]
    cosine, sine = jnp.cos(angles), jnp.sin(angles)
    one, zero = jnp.ones((16, HD), F32), jnp.zeros((16, HD), F32)
    cosine = jnp.concatenate([cosine] * 4 + [one], axis=1)[:, None, :]
    sine = jnp.concatenate([-sine, sine] * 2 + [zero], axis=1)[:, None, :]

    pairs = []
    for f in range(16):
        turn = f % 2 * 2 + f // 8
        for t in range(16):
            head = (t // 4 + turn) % 4 * 4 + (t + f // 2 % 4 + turn) % 4
            pairs.append((f * 16 + head, f * 16 + t))
    head_a = lax.ppermute(jnp.concatenate([w_tqkv.T, w_to], axis=0), ("frame", "tensor"), pairs)

    def in_ring_order(v):
        v = v.reshape(4, 4, HD, -1).transpose(1, 0, 2, 3)
        v = lax.dynamic_slice_in_dim(jnp.concatenate([v, v], axis=0), x, 4, 0)
        n = v.shape[-1]
        parts = [v[:, :, :40].reshape(4, 160, n), v[:, :, 40:].reshape(4, 128, n)]
        return jnp.concatenate(parts, axis=1).reshape(D, n)

    weight = in_ring_order(w_sqkv).T.reshape(3, HD, D)
    weight = jnp.pad(weight, ((0, 0), (0, PAD - HD), (0, 0))).reshape(3 * PAD, D)
    shift_scale = in_ring_order(modulation[:2].T).T
    shift_scale = jnp.concatenate([shift_scale, jnp.zeros((6, D), F32)], axis=0)
    pieces, late, cosine, sine, weight, shift_scale, modulation = together(
        (pieces, late, cosine, sine, weight, shift_scale, modulation)
    )

    so_half = lax.all_gather(
        late[:, 2 * D :], "tensor", axis=0, tiled=True, axis_index_groups=x_groups
    )
    attended = spatial_attention(pieces, weight, shift_scale)
    stream = jnp.concatenate(
        [stream_top.reshape(4, 4, 40, ROWS), stream_low.reshape(4, 4, 32, ROWS)], axis=2
    )
    stream = row_major(stream.transpose(1, 0, 2, 3).reshape(D, ROWS).T)
    attended, late, head_a = together((attended, late, head_a))
    fc_all = lax.all_gather(
        late[:, : 2 * D], "tensor", axis=0, tiled=True, axis_index_groups=x_groups
    )
    head_b = move_frame(head_a, dzl=1)
    attended = lax.all_to_all(attended, "tensor", split_axis=1, concat_axis=0, tiled=True)
    so_half = so_half.reshape(4, 4, HD, D // 2).transpose(1, 0, 2, 3).reshape(D, D // 2)
    attended = jnp.concatenate([attended, move_frame(attended, dcore=1)], axis=1)
    mine = dot(attended, so_half, ((0,), (0,))).astype(BF16)
    theirs = move_frame(mine[ROWS:], dcore=1)
    mine = mine[:ROWS]
    projected = jnp.where(
        core == 0, jnp.concatenate([mine, theirs], axis=1), jnp.concatenate([theirs, mine], axis=1)
    ).astype(F32)
    stream = row_major((stream.astype(F32) + modulation[2] * projected).astype(BF16))

    rows = gather_rows(branch_input(stream, modulation[3], modulation[4]))
    qkv_b = dot(rows, head_b[: 3 * HD], ((1,), (1,))).astype(BF16)
    qkv_b = move_frame(qkv_b, dzl=1)
    qkv_a = dot(rows, head_a[: 3 * HD], ((1,), (1,))).astype(BF16)
    out_a, out_b = temporal_attention(qkv_a, qkv_b, cosine, sine)
    out_b = move_frame(out_b, dzl=1)
    partial = dot(out_a, head_a[3 * HD :]) + dot(out_b, head_b[3 * HD :])
    partial, fc_all = together((row_major(partial.astype(BF16)), fc_all))
    stream = row_major((stream.astype(F32) + modulation[5] * scatter_rows(partial)).astype(BF16))

    rows = branch_input(stream, modulation[6], modulation[7])
    rows = jnp.concatenate([rows, move_frame(rows, dzl=1)], axis=0)
    rows = jnp.concatenate([rows, move_frame(rows, dcore=1)], axis=0)
    partial = mlp(rows, fc_all)
    partial = partial[: 2 * ROWS].astype(F32) + move_frame(partial[2 * ROWS :], dcore=1).astype(F32)
    partial = partial[:ROWS] + move_frame(partial[ROWS:].astype(BF16), dzl=1).astype(F32)
    stream = stream.astype(F32) + modulation[8] * partial
    return lax.all_to_all(stream.astype(BF16), "tensor", split_axis=1, concat_axis=0, tiled=True)


def solution(mesh):
    placed = (
        P("frame", "tensor"),
        P(),
        P("frame"),
        P(),
        P(None, "tensor"),
        P("tensor", None),
        P(None, "tensor"),
        P("tensor", None),
        P(None, "tensor"),
        P("tensor", None),
        P(None, "tensor"),
        P("tensor", None),
    )
    return jax.shard_map(
        shards, mesh=mesh, in_specs=placed, out_specs=P("frame", "tensor"), check_vma=False
    )
```

```python
import math

import jax
import jax.numpy as jnp
from jax import lax
from jax.experimental import pallas as pl
from jax.experimental.layout import Layout, with_layout_constraint
from jax.experimental.pallas import tpu as pltpu
from jax.sharding import PartitionSpec as P

D = 1152
HD = 72
P_SIZE = 1920
N_T = 16
ROWS = P_SIZE // N_T
FF_PART = 72
SCALE_LOG2 = HD ** (-0.5) * math.log2(math.e)
Q_BLOCK = 384
PAD = 80
BLOCK = 128
F32 = jnp.float32
BF16 = jnp.bfloat16


def layer_norm(values_in):
    center = values_in - jnp.mean(values_in, axis=-1, keepdims=True)
    spread = jnp.mean(center * center, axis=-1, keepdims=True)
    return center * lax.rsqrt(spread + 1e-06)


def branch_input(stream, shift, scale):
    return (layer_norm(stream.astype(F32)) * (1.0 + scale) + shift).astype(BF16)


def time_features(timestep, width):
    half_width = width // 2
    frequency = jnp.exp(-math.log(10000.0) * jnp.arange(half_width, dtype=F32) / half_width)
    angles = timestep.astype(F32)[:, None] * frequency[None, :]
    return jnp.concatenate([jnp.cos(angles), jnp.sin(angles)], axis=1).astype(BF16)


def dot(a, b, contract=((1,), (0,))):
    return lax.dot_general(a, b, (contract, ((), ())), preferred_element_type=F32)


def row_major(v):
    return with_layout_constraint(v, Layout(major_to_minor=tuple(range(v.ndim))))


def move_frame(v, dzl=0, dy=0, dcore=0):
    pairs = []
    for source in range(16):
        zl, y, core = source // 8, source // 2 % 4, source % 2
        pairs.append((source, (zl ^ dzl) * 8 + (y + dy) % 4 * 2 + (core ^ dcore)))
    return lax.ppermute(v, "frame", pairs)


def move_tensor(v, dzh=0, dx=0):
    pairs = []
    for source in range(16):
        zh, x = source // 4, source % 4
        pairs.append((source, (zh + dzh) % 4 * 4 + (x + dx) % 4))
    return lax.ppermute(v, "tensor", pairs)


def ring(own, move, half):
    return ring_far(own, move(own, 1), move(own, -1), move, half)


def ring_far(own, before, after, move, half):
    return own, after, move(before[:half], 1), move(after[half:], -1), before


def ring_in_halves(top, low, move):
    before_top, after_low = move(top, 1), move(low, -1)
    before_low, after_top = move(low, 1), move(top, -1)
    far_top, far_low = move(before_top, 1), move(after_low, -1)
    return (top, low), (after_top, after_low), (far_top, far_low), (before_top, before_low)


def placed_rows(blocks, rows, position, steps=(0, 1, 2, 3), out=None):
    if out is None:
        out = jnp.zeros((4, rows[1] - rows[0]) + blocks[0][0].shape[1:], blocks[0][0].dtype)
    for step in steps:
        parts = blocks[step]
        start = 0
        for part in parts:
            stop = start + part.shape[0]
            low, high = max(start, rows[0]), min(stop, rows[1])
            if low < high:
                piece = part[low - start : high - start][None]
                out = lax.dynamic_update_slice(out, piece, ((position + step) % 4, low - rows[0], 0))
            start = stop
    return out


def along_zh(v, d):
    return move_tensor(v, dzh=d)


def along_x(v, d):
    return move_tensor(v, dx=d)


def along_y(v, d):
    return move_frame(v, dy=d)


def gather_column(own):
    return row_major(jnp.concatenate(ring(row_major(own), along_y, 64), axis=0))


def scatter_rows(partial):
    half = 64
    n = partial.shape[0] // 2
    column = partial[:n].astype(F32) + move_frame(partial[n:], dcore=1).astype(F32)
    blocks = column.reshape(4, n // 4, partial.shape[1])
    own, sent = blocks[0], blocks.astype(BF16)
    far_a, far_b = along_y(sent[2, :half], 1), along_y(sent[2, half:], -1)
    up, down = along_y(sent[1], 1), along_y(sent[3], -1)
    far = jnp.concatenate([along_y(far_a, 1), along_y(far_b, -1)], axis=0)
    return own + up.astype(F32) + down.astype(F32) + far.astype(F32)


def spatial_kernel(*refs):
    pieces, (weight_ref, shift_scale_ref, out_ref, queries, keys, values) = refs[:8], refs[8:]

    @pl.when(pl.program_id(0) == 0)
    def _():
        shift_scale = shift_scale_ref[...].T
        shift, scale = shift_scale[:, 0:1], 1.0 + shift_scale[:, 1:2]
        ones_row = lax.broadcasted_iota(jnp.int32, (PAD, Q_BLOCK), 0) == HD
        for part in range(P_SIZE // Q_BLOCK):
            columns = slice(part * Q_BLOCK, (part + 1) * Q_BLOCK)
            rows = [ref[:, columns] for ref in pieces]
            features = jnp.concatenate(rows, axis=0).astype(F32)
            center = features - jnp.mean(features, axis=0, keepdims=True)
            spread = jnp.mean(center * center, axis=0, keepdims=True)
            normed = center * lax.rsqrt(spread + 1e-06) * scale + shift
            qkv = dot(weight_ref[...], normed.astype(BF16))
            queries[:, columns] = qkv[:PAD].astype(BF16)
            keys[columns, :] = qkv[PAD : 2 * PAD].T.astype(BF16)
            values[:, columns] = jnp.where(ones_row, 1.0, qkv[2 * PAD :]).astype(BF16)

    start = pl.multiple_of(pl.program_id(0) * Q_BLOCK, 128)
    scores = dot(keys[...], queries[:, pl.ds(start, Q_BLOCK)])
    top = jnp.max(scores, axis=0, keepdims=True)
    weights = jnp.exp2((scores - top) * SCALE_LOG2).astype(BF16)
    summed = dot(values[...], weights)
    out_ref[...] = (summed[:HD] / summed[HD : HD + 1]).astype(BF16)


def spatial_attention(pieces, weight, shift_scale):
    whole = lambda v: pl.BlockSpec(v.shape, lambda i: (0, 0))
    operands = (*pieces, weight, shift_scale)
    return pl.pallas_call(
        spatial_kernel,
        grid=(P_SIZE // Q_BLOCK,),
        out_shape=jax.ShapeDtypeStruct((HD, P_SIZE), BF16),
        in_specs=[whole(v) for v in operands],
        out_specs=pl.BlockSpec((HD, Q_BLOCK), lambda i: (0, i)),
        scratch_shapes=[
            pltpu.VMEM((PAD, P_SIZE), BF16),
            pltpu.VMEM((P_SIZE, PAD), BF16),
            pltpu.VMEM((PAD, P_SIZE), BF16),
        ],
        compiler_params=pltpu.CompilerParams(vmem_limit_bytes=48 * 2**20),
        cost_estimate=pl.CostEstimate(
            flops=4 * P_SIZE * P_SIZE * HD + 2 * P_SIZE * D * 3 * HD,
            bytes_accessed=P_SIZE * D * 2,
            transcendentals=P_SIZE * P_SIZE,
        ),
    )(*operands)


def mlp_kernel(rows_ref, weight_ref, out_ref):
    total = jnp.zeros(out_ref.shape, F32)
    step = 384
    for start in range(0, D, step):
        units = slice(start, start + step)
        hidden = dot(rows_ref[...], weight_ref[units, :D], ((1,), (1,)))
        hidden = jax.nn.gelu(hidden, approximate=True).astype(BF16)
        total = total + dot(hidden, weight_ref[units, D:])
    out_ref[...] = total.astype(BF16)


def mlp(rows, weight):
    return pl.pallas_call(
        mlp_kernel,
        out_shape=jax.ShapeDtypeStruct(rows.shape, BF16),
        compiler_params=pltpu.CompilerParams(vmem_limit_bytes=40 * 2**20),
        cost_estimate=pl.CostEstimate(
            flops=4 * rows.shape[0] * D * D, bytes_accessed=6 * D * D, transcendentals=rows.shape[0] * D
        ),
    )(rows, weight)


def rotated_kernel(rows_ref, weight_ref, swap_ref, out_ref):
    projected = dot(rows_ref[...], weight_ref[...], ((1,), (1,))).astype(BF16)
    swapped = dot(projected, swap_ref[...])
    projected = projected.astype(F32)
    for frame in range(8):
        rows = slice(BLOCK * frame, BLOCK * frame + BLOCK)
        table = rows_ref[BLOCK * frame + BLOCK - 16 : BLOCK * frame + BLOCK, : 3 * HD].astype(F32)
        cosine, sine = table[8:9] + table[9:10], table[10:11] + table[11:12]
        out_ref[rows] = (projected[rows] * cosine + swapped[rows] * sine).astype(BF16)


def rotated_qkv(rows, weight):
    lane = jnp.arange(3 * HD)
    half = HD // 2
    partner = jnp.where(lane % HD < half, lane + half, lane - half)
    swap = ((lane[:, None] == partner[None, :]) & (lane[None, :] < 2 * HD)).astype(BF16)
    return pl.pallas_call(
        rotated_kernel,
        out_shape=jax.ShapeDtypeStruct((8 * BLOCK, 3 * HD), BF16),
        compiler_params=pltpu.CompilerParams(vmem_limit_bytes=32 * 2**20),
        cost_estimate=pl.CostEstimate(
            flops=16 * BLOCK * D * 3 * HD, bytes_accessed=16 * BLOCK * D, transcendentals=0
        ),
    )(rows, weight, swap)


def rotation_table(position):
    half = HD // 2
    frequency = jnp.exp(-math.log(10000.0) * jnp.arange(half, dtype=F32) / half)
    angles = position.astype(F32) * frequency
    cosine, sine = jnp.cos(angles), jnp.sin(angles)
    cosine = jnp.concatenate([cosine] * 4 + [jnp.ones((HD,), F32)])
    sine = jnp.concatenate([-sine, sine] * 2 + [jnp.zeros((HD,), F32)])
    rows = []
    for values in (cosine, sine):
        high = lax.reduce_precision(values, 8, 7)
        rows += [high.astype(BF16), (values - high).astype(BF16)]
    return jnp.pad(jnp.stack(rows), ((0, 4), (0, D - 3 * HD)))


def temporal_kernel(own_ref, other_ref, out_own_ref, out_other_ref):
    row = lax.broadcasted_iota(jnp.int32, (256, 256), 0)
    column = lax.broadcasted_iota(jnp.int32, (256, 256), 1)
    same = (row % 16) == (column % 16)
    for group in range(BLOCK // 16):
        rows = [slice(BLOCK * frame + 16 * group, BLOCK * frame + 16 * group + 16) for frame in range(8)]
        section = jnp.concatenate([ref[r, :] for ref in (own_ref, other_ref) for r in rows], axis=0)
        queries, keys, values = section[:, :HD], section[:, HD : 2 * HD], section[:, 2 * HD :]
        scores = jnp.where(same, dot(queries, keys, ((1,), (1,))), -jnp.inf)
        top = jnp.max(scores, axis=1, keepdims=True)
        weights = jnp.exp2((scores - top) * SCALE_LOG2)
        weights = (weights / jnp.sum(weights, axis=1, keepdims=True)).astype(BF16)
        result = dot(weights, values).astype(BF16)
        for index, r in enumerate(rows):
            out_own_ref[r, :] = result[16 * index : 16 * index + 16]
            out_other_ref[r, :] = result[128 + 16 * index : 144 + 16 * index]


def temporal_attention(own, other):
    shape = jax.ShapeDtypeStruct((8 * BLOCK, HD), BF16)
    return pl.pallas_call(
        temporal_kernel,
        out_shape=(shape, shape),
        compiler_params=pltpu.CompilerParams(vmem_limit_bytes=32 * 2**20),
        cost_estimate=pl.CostEstimate(
            flops=16 * BLOCK * 256 * HD * 4, bytes_accessed=16 * BLOCK * HD * 8, transcendentals=16 * BLOCK * 256
        ),
    )(own, other)


def shards(
    latent, timestep, frame_pos, time_w1, time_w2, ada_w, w_sqkv, w_so, w_tqkv, w_to, w_fc1, w_fc2
):
    frame = lax.axis_index("frame")
    tensor = lax.axis_index("tensor")
    zl, y, core = frame // 8, frame // 2 % 4, frame % 2

    zh, x = tensor // 4, tensor % 4
    together = lax.optimization_barrier

    zh_groups = [[4 * i + j for i in range(4)] for j in range(4)]
    x_groups = [[4 * i + j for j in range(4)] for i in range(4)]

    own = latent.T
    before, after, w_fc1, w_fc2, w_so = together(
        (along_zh(own, 1), along_zh(own, -1), w_fc1, w_fc2, w_so)
    )
    own, after, far_top, far_low, before = ring_far(own, before, after, along_zh, 40)
    blocks = (own,), (after,), (far_top, far_low), (before,)
    latent_top = placed_rows(blocks, (0, 40), zh).reshape(160, P_SIZE)
    latent_low = placed_rows(blocks, (40, HD), zh).reshape(128, P_SIZE)

    part = (zl * 2 + core) * FF_PART
    late = jnp.concatenate(
        [
            lax.dynamic_slice_in_dim(w_fc1, part, FF_PART, 1).T,
            lax.dynamic_slice_in_dim(w_fc2, part, FF_PART, 0),
            lax.dynamic_slice_in_dim(w_so, core * (D // 2), D // 2, 1),
        ],
        axis=1,
    )

    time_embed = time_features(timestep, time_w1.shape[0])
    hidden_time = jax.nn.silu(dot(time_embed, time_w1)).astype(BF16)
    condition = jax.nn.silu(dot(hidden_time, time_w2)).astype(BF16)
    terms = dot(condition, ada_w).astype(BF16).reshape(1, 9, D)
    table = rotation_table(frame_pos)
    latent_top, latent_low, w_sqkv, terms, table = together(
        (latent_top, latent_low, w_sqkv, terms, table)
    )
    terms = lax.all_to_all(jnp.broadcast_to(terms, (N_T, 9, D)), "tensor", 0, 0)
    late = lax.all_gather(late, "tensor", axis=0, tiled=True, axis_index_groups=zh_groups)
    blocks = ring_in_halves(latent_top, latent_low, along_x)
    modulation = jnp.sum(terms.astype(F32), axis=0)
    pieces = [part for block in blocks for part in block]
    stream = [[lax.dynamic_slice_in_dim(p, tensor * ROWS, ROWS, 1) for p in block] for block in blocks]
    tops, lows = [(block[0],) for block in stream], [(block[1],) for block in stream]
    stream_top = placed_rows(tops, (0, 160), x, (0, 1, 3))
    stream_low = placed_rows(lows, (0, 128), x, (0, 1, 3))
    def in_ring_order(v):
        v = v.reshape(4, 4, HD, -1).transpose(1, 0, 2, 3)
        v = lax.dynamic_slice_in_dim(jnp.concatenate([v, v], axis=0), x, 4, 0)
        n = v.shape[-1]
        parts = [v[:, :, :40].reshape(4, 160, n), v[:, :, 40:].reshape(4, 128, n)]
        return jnp.concatenate(parts, axis=1).reshape(D, n)

    weight = in_ring_order(w_sqkv).T.reshape(3, HD, D)
    weight = jnp.pad(weight, ((0, 0), (0, PAD - HD), (0, 0))).reshape(3 * PAD, D)
    shift_scale = in_ring_order(modulation[:2].T).T
    shift_scale = jnp.concatenate([shift_scale, jnp.zeros((6, D), F32)], axis=0)
    pieces, late, weight, shift_scale, modulation, stream_top, stream_low, w_tqkv, w_to = together(
        (pieces, late, weight, shift_scale, modulation, stream_top, stream_low, w_tqkv, w_to)
    )

    pairs = []
    for f in range(16):
        turn = f % 2 * 2 + f // 8
        for t in range(16):
            head = (t // 4 + turn) % 4 * 4 + (t + f // 2 % 4 + turn) % 4
            pairs.append((f * 16 + head, f * 16 + t))
    head_a = lax.ppermute(jnp.concatenate([w_tqkv.T, w_to], axis=0), ("frame", "tensor"), pairs)

    so_half = lax.all_gather(
        late[:, 2 * D :], "tensor", axis=0, tiled=True, axis_index_groups=x_groups
    )
    attended = spatial_attention(pieces, weight, shift_scale)
    stream_top = placed_rows(tops, (0, 160), x, (2,), stream_top)
    stream_low = placed_rows(lows, (0, 128), x, (2,), stream_low)
    stream = jnp.concatenate(
        [stream_top.reshape(4, 4, 40, ROWS), stream_low.reshape(4, 4, 32, ROWS)], axis=2
    )
    stream = row_major(stream.transpose(1, 0, 2, 3).reshape(D, ROWS).T)
    attended, late, head_a = together((attended, late, head_a))
    fc_all = lax.all_gather(
        late[:, : 2 * D], "tensor", axis=0, tiled=True, axis_index_groups=x_groups
    )
    attended = lax.all_to_all(attended, "tensor", split_axis=1, concat_axis=0, tiled=True)
    attended = attended.reshape(4, 4, HD, ROWS).transpose(1, 0, 2, 3).reshape(D, ROWS)
    attended = jnp.concatenate([attended, move_frame(attended, dcore=1)], axis=1)
    mine = dot(attended, so_half, ((0,), (0,))).astype(BF16)
    theirs = move_frame(mine[ROWS:], dcore=1)
    mine = mine[:ROWS]
    projected = jnp.where(
        core == 0, jnp.concatenate([mine, theirs], axis=1), jnp.concatenate([theirs, mine], axis=1)
    ).astype(F32)
    stream = row_major((stream.astype(F32) + modulation[2] * projected).astype(BF16))

    rows = jnp.concatenate([branch_input(stream, modulation[3], modulation[4]), table], axis=0)
    head_b = move_frame(head_a, dzl=1)
    column, head_b = together((gather_column(rows), head_b))
    rows = row_major(jnp.concatenate([column, move_frame(column, dcore=1)], axis=0))
    qkv_b = move_frame(rotated_qkv(rows, head_b[: 3 * HD]), dzl=1)
    qkv_a = rotated_qkv(rows, head_a[: 3 * HD])
    out_a, out_b = temporal_attention(qkv_a, qkv_b)
    out_b = move_frame(out_b, dzl=1)
    out = jnp.concatenate([out_a, out_b], axis=1)
    w_out = jnp.concatenate([head_a[3 * HD :], head_b[3 * HD :]], axis=0)
    partial = row_major(dot(out, w_out).astype(BF16))
    partial, fc_all = together((partial, fc_all))
    stream = row_major((stream.astype(F32) + modulation[5] * scatter_rows(partial)[:ROWS]).astype(BF16))

    rows = branch_input(stream, modulation[6], modulation[7])
    rows = jnp.concatenate([rows, move_frame(rows, dzl=1)], axis=0)
    rows = jnp.concatenate([rows, move_frame(rows, dcore=1)], axis=0)
    partial = mlp(rows, fc_all)
    partial = partial[: 2 * ROWS].astype(F32) + move_frame(partial[2 * ROWS :], dcore=1).astype(F32)
    partial = partial[:ROWS] + move_frame(partial[ROWS:].astype(BF16), dzl=1).astype(F32)
    stream = stream.astype(F32) + modulation[8] * partial
    return lax.all_to_all(stream.astype(BF16), "tensor", split_axis=1, concat_axis=0, tiled=True)


def solution(mesh):
    placed = (
        P("frame", "tensor"),
        P(),
        P("frame"),
        P(),
        P(None, "tensor"),
        P("tensor", None),
        P(None, "tensor"),
        P("tensor", None),
        P(None, "tensor"),
        P("tensor", None),
        P(None, "tensor"),
        P("tensor", None),
    )
    return jax.shard_map(
        shards, mesh=mesh, in_specs=placed, out_specs=P("frame", "tensor"), check_vma=False
    )
```

```python
import math

import jax
import jax.numpy as jnp
from jax import lax
from jax.experimental import pallas as pl
from jax.experimental.layout import Layout, with_layout_constraint
from jax.experimental.pallas import tpu as pltpu
from jax.sharding import PartitionSpec as P

D = 1152
HD = 72
P_SIZE = 1920
N_T = 16
ROWS = P_SIZE // N_T
FF_PART = 72
SCALE_LOG2 = HD ** (-0.5) * math.log2(math.e)
Q_BLOCK = 384
PAD = 80
BLOCK = 128
F32 = jnp.float32
BF16 = jnp.bfloat16


def layer_norm(values_in):
    center = values_in - jnp.mean(values_in, axis=-1, keepdims=True)
    spread = jnp.mean(center * center, axis=-1, keepdims=True)
    return center * lax.rsqrt(spread + 1e-06)


def branch_input(stream, shift, scale):
    return (layer_norm(stream.astype(F32)) * (1.0 + scale) + shift).astype(BF16)


def time_features(timestep, width):
    half_width = width // 2
    frequency = jnp.exp(-math.log(10000.0) * jnp.arange(half_width, dtype=F32) / half_width)
    angles = timestep.astype(F32)[:, None] * frequency[None, :]
    return jnp.concatenate([jnp.cos(angles), jnp.sin(angles)], axis=1).astype(BF16)


def dot(a, b, contract=((1,), (0,))):
    return lax.dot_general(a, b, (contract, ((), ())), preferred_element_type=F32)


def row_major(v):
    return with_layout_constraint(v, Layout(major_to_minor=tuple(range(v.ndim))))


def move_frame(v, dzl=0, dy=0, dcore=0):
    pairs = []
    for source in range(16):
        zl, y, core = source // 8, source // 2 % 4, source % 2
        pairs.append((source, (zl ^ dzl) * 8 + (y + dy) % 4 * 2 + (core ^ dcore)))
    return lax.ppermute(v, "frame", pairs)


def move_tensor(v, dzh=0, dx=0):
    pairs = []
    for source in range(16):
        zh, x = source // 4, source % 4
        pairs.append((source, (zh + dzh) % 4 * 4 + (x + dx) % 4))
    return lax.ppermute(v, "tensor", pairs)


def ring(own, move, half):
    return ring_far(own, move(own, 1), move(own, -1), move, half)


def ring_far(own, before, after, move, half):
    return own, after, move(before[:half], 1), move(after[half:], -1), before


def ring_in_halves(top, low, move):
    before_top, after_low = move(top, 1), move(low, -1)
    before_low, after_top = move(low, 1), move(top, -1)
    far_top, far_low = move(before_top, 1), move(after_low, -1)
    return (top, low), (after_top, after_low), (far_top, far_low), (before_top, before_low)


def placed_rows(blocks, rows, position, steps=(0, 1, 2, 3), out=None):
    if out is None:
        out = jnp.zeros((4, rows[1] - rows[0]) + blocks[0][0].shape[1:], blocks[0][0].dtype)
    for step in steps:
        parts = blocks[step]
        start = 0
        for part in parts:
            stop = start + part.shape[0]
            low, high = max(start, rows[0]), min(stop, rows[1])
            if low < high:
                piece = part[low - start : high - start][None]
                out = lax.dynamic_update_slice(out, piece, ((position + step) % 4, low - rows[0], 0))
            start = stop
    return out


def along_zh(v, d):
    return move_tensor(v, dzh=d)


def along_x(v, d):
    return move_tensor(v, dx=d)


def along_y(v, d):
    return move_frame(v, dy=d)


def gather_column(own, y):
    own, after, far_a, far_b, before = ring(row_major(own), along_y, 64)
    column = placed_rows(((own,), (after,), (far_a, far_b), (before,)), (0, BLOCK), y)
    return row_major(column.reshape(4 * BLOCK, D))


def scatter_rows(partial):
    n = partial.shape[0] // 2
    column = partial[:n].astype(F32) + move_frame(partial[n:], dcore=1).astype(F32)
    blocks = column.astype(BF16).reshape(4, n // 4, partial.shape[1])
    groups = [[8 * zl + 2 * y + core for y in range(4)] for zl in range(2) for core in range(2)]
    terms = lax.all_to_all(blocks, "frame", 0, 0, axis_index_groups=groups)
    return jnp.sum(terms.astype(F32), axis=0)


def spatial_kernel(*refs):
    pieces, (weight_ref, shift_scale_ref, out_ref, queries, keys, values) = refs[:8], refs[8:]

    shift_scale = shift_scale_ref[...].T
    shift, scale = shift_scale[:, 0:1], 1.0 + shift_scale[:, 1:2]
    ones_row = lax.broadcasted_iota(jnp.int32, (PAD, Q_BLOCK), 0) == HD
    parts = [slice(start, start + Q_BLOCK) for start in range(0, P_SIZE, Q_BLOCK)]
    for part in parts:
        rows = [ref[:, part] for ref in pieces]
        features = jnp.concatenate(rows, axis=0).astype(F32)
        center = features - jnp.mean(features, axis=0, keepdims=True)
        spread = jnp.mean(center * center, axis=0, keepdims=True)
        normed = center * lax.rsqrt(spread + 1e-06) * scale + shift
        qkv = dot(weight_ref[...], normed.astype(BF16))
        queries[:, part] = qkv[:PAD].astype(BF16)
        keys[part, :] = qkv[PAD : 2 * PAD].T.astype(BF16)
        values[:, part] = jnp.where(ones_row, 1.0, qkv[2 * PAD :]).astype(BF16)

    top = total = None
    for part in parts:
        scores = dot(keys[part, :], queries[...])
        block_top = jnp.max(scores, axis=0, keepdims=True) * SCALE_LOG2
        new_top = block_top if top is None else jnp.maximum(top, block_top)
        weights = jnp.exp2(scores * SCALE_LOG2 - new_top).astype(BF16)
        term = dot(values[:, part], weights)
        total = term if top is None else total * jnp.exp2(top - new_top) + term
        top = new_top
    out_ref[...] = (total[:HD] / total[HD : HD + 1]).astype(BF16)


def spatial_attention(pieces, weight, shift_scale):
    operands = (*pieces, weight, shift_scale)
    return pl.pallas_call(
        spatial_kernel,
        out_shape=jax.ShapeDtypeStruct((HD, P_SIZE), BF16),
        scratch_shapes=[
            pltpu.VMEM((PAD, P_SIZE), BF16),
            pltpu.VMEM((P_SIZE, PAD), BF16),
            pltpu.VMEM((PAD, P_SIZE), BF16),
        ],
        compiler_params=pltpu.CompilerParams(vmem_limit_bytes=48 * 2**20),
        cost_estimate=pl.CostEstimate(
            flops=4 * P_SIZE * P_SIZE * HD + 2 * P_SIZE * D * 3 * HD,
            bytes_accessed=P_SIZE * D * 2,
            transcendentals=P_SIZE * P_SIZE,
        ),
    )(*operands)


def mlp_kernel(rows_ref, weight_ref, out_ref):
    total = jnp.zeros(out_ref.shape, F32)
    step = 384
    for start in range(0, D, step):
        units = slice(start, start + step)
        hidden = dot(rows_ref[...], weight_ref[units, :D], ((1,), (1,)))
        hidden = jax.nn.gelu(hidden, approximate=True).astype(BF16)
        total = total + dot(hidden, weight_ref[units, D:])
    out_ref[...] = total.astype(BF16)


def mlp(rows, weight):
    return pl.pallas_call(
        mlp_kernel,
        out_shape=jax.ShapeDtypeStruct(rows.shape, BF16),
        compiler_params=pltpu.CompilerParams(vmem_limit_bytes=40 * 2**20),
        cost_estimate=pl.CostEstimate(
            flops=4 * rows.shape[0] * D * D, bytes_accessed=6 * D * D, transcendentals=rows.shape[0] * D
        ),
    )(rows, weight)


def rotated_kernel(rows_ref, weight_ref, swap_ref, out_ref):
    projected = dot(rows_ref[...], weight_ref[...], ((1,), (1,))).astype(BF16)
    swapped = dot(projected, swap_ref[...])
    projected = projected.astype(F32)
    for frame in range(8):
        rows = slice(BLOCK * frame, BLOCK * frame + BLOCK)
        table = rows_ref[BLOCK * frame + BLOCK - 16 : BLOCK * frame + BLOCK, : 3 * HD].astype(F32)
        cosine, sine = table[8:9] + table[9:10], table[10:11] + table[11:12]
        out_ref[rows] = (projected[rows] * cosine + swapped[rows] * sine).astype(BF16)


def rotated_qkv(rows, weight):
    lane = jnp.arange(3 * HD)
    half = HD // 2
    partner = jnp.where(lane % HD < half, lane + half, lane - half)
    swap = ((lane[:, None] == partner[None, :]) & (lane[None, :] < 2 * HD)).astype(BF16)
    return pl.pallas_call(
        rotated_kernel,
        out_shape=jax.ShapeDtypeStruct((8 * BLOCK, 3 * HD), BF16),
        compiler_params=pltpu.CompilerParams(vmem_limit_bytes=32 * 2**20),
        cost_estimate=pl.CostEstimate(
            flops=16 * BLOCK * D * 3 * HD, bytes_accessed=16 * BLOCK * D, transcendentals=0
        ),
    )(rows, weight, swap)


def rotation_table(position):
    half = HD // 2
    frequency = jnp.exp(-math.log(10000.0) * jnp.arange(half, dtype=F32) / half)
    angles = position.astype(F32) * frequency
    cosine, sine = jnp.cos(angles), jnp.sin(angles)
    cosine = jnp.concatenate([cosine] * 4 + [jnp.ones((HD,), F32)])
    sine = jnp.concatenate([-sine, sine] * 2 + [jnp.zeros((HD,), F32)])
    rows = []
    for values in (cosine, sine):
        high = lax.reduce_precision(values, 8, 7)
        rows += [high.astype(BF16), (values - high).astype(BF16)]
    return jnp.pad(jnp.stack(rows), ((0, 4), (0, D - 3 * HD)))


def temporal_kernel(own_ref, other_ref, out_own_ref, out_other_ref):
    row = lax.broadcasted_iota(jnp.int32, (256, 256), 0)
    column = lax.broadcasted_iota(jnp.int32, (256, 256), 1)
    same = (row % 16) == (column % 16)
    for group in range(BLOCK // 16):
        rows = [slice(BLOCK * frame + 16 * group, BLOCK * frame + 16 * group + 16) for frame in range(8)]
        section = jnp.concatenate([ref[r, :] for ref in (own_ref, other_ref) for r in rows], axis=0)
        queries, keys, values = section[:, :HD], section[:, HD : 2 * HD], section[:, 2 * HD :]
        scores = jnp.where(same, dot(queries, keys, ((1,), (1,))), -jnp.inf)
        top = jnp.max(scores, axis=1, keepdims=True)
        weights = jnp.exp2((scores - top) * SCALE_LOG2)
        weights = (weights / jnp.sum(weights, axis=1, keepdims=True)).astype(BF16)
        result = dot(weights, values).astype(BF16)
        for index, r in enumerate(rows):
            out_own_ref[r, :] = result[16 * index : 16 * index + 16]
            out_other_ref[r, :] = result[128 + 16 * index : 144 + 16 * index]


def temporal_attention(own, other):
    shape = jax.ShapeDtypeStruct((8 * BLOCK, HD), BF16)
    return pl.pallas_call(
        temporal_kernel,
        out_shape=(shape, shape),
        compiler_params=pltpu.CompilerParams(vmem_limit_bytes=32 * 2**20),
        cost_estimate=pl.CostEstimate(
            flops=16 * BLOCK * 256 * HD * 4, bytes_accessed=16 * BLOCK * HD * 8, transcendentals=16 * BLOCK * 256
        ),
    )(own, other)


def shards(
    latent, timestep, frame_pos, time_w1, time_w2, ada_w, w_sqkv, w_so, w_tqkv, w_to, w_fc1, w_fc2
):
    frame = lax.axis_index("frame")
    tensor = lax.axis_index("tensor")
    zl, y, core = frame // 8, frame // 2 % 4, frame % 2

    zh, x = tensor // 4, tensor % 4
    together = lax.optimization_barrier

    zh_groups = [[4 * i + j for i in range(4)] for j in range(4)]
    x_groups = [[4 * i + j for j in range(4)] for i in range(4)]

    pairs = []
    for f in range(16):
        turn = f % 2 * 2 + f // 8
        for t in range(16):
            head = (t // 4 + turn) % 4 * 4 + (t + f // 2 % 4 + turn) % 4
            pairs.append((f * 16 + head, f * 16 + t))
    head_a = lax.ppermute(jnp.concatenate([w_tqkv.T, w_to], axis=0), ("frame", "tensor"), pairs)

    own = latent.T
    before, after, w_fc1, w_fc2, w_so = together(
        (along_zh(own, 1), along_zh(own, -1), w_fc1, w_fc2, w_so)
    )
    own, after, far_top, far_low, before = ring_far(own, before, after, along_zh, 40)
    blocks = (own,), (after,), (far_top, far_low), (before,)
    latent_top = placed_rows(blocks, (0, 40), zh).reshape(160, P_SIZE)
    latent_low = placed_rows(blocks, (40, HD), zh).reshape(128, P_SIZE)

    part = (zl * 2 + core) * FF_PART
    late = jnp.concatenate(
        [
            lax.dynamic_slice_in_dim(w_fc1, part, FF_PART, 1).T,
            lax.dynamic_slice_in_dim(w_fc2, part, FF_PART, 0),
            lax.dynamic_slice_in_dim(w_so, core * (D // 2), D // 2, 1),
        ],
        axis=1,
    )

    time_embed = time_features(timestep, time_w1.shape[0])
    hidden_time = jax.nn.silu(dot(time_embed, time_w1)).astype(BF16)
    condition = jax.nn.silu(dot(hidden_time, time_w2)).astype(BF16)
    terms = dot(condition, ada_w).astype(BF16).reshape(1, 9, D)
    table = rotation_table(frame_pos)
    latent_top, latent_low, w_sqkv, terms, table, head_a = together(
        (latent_top, latent_low, w_sqkv, terms, table, head_a)
    )
    terms = lax.all_to_all(jnp.broadcast_to(terms, (N_T, 9, D)), "tensor", 0, 0)
    late = lax.all_gather(late, "tensor", axis=0, tiled=True, axis_index_groups=zh_groups)
    blocks = ring_in_halves(latent_top, latent_low, along_x)
    modulation = jnp.sum(terms.astype(F32), axis=0)
    pieces = [part for block in blocks for part in block]
    stream = [[lax.dynamic_slice_in_dim(p, tensor * ROWS, ROWS, 1) for p in block] for block in blocks]
    tops, lows = [(block[0],) for block in stream], [(block[1],) for block in stream]
    stream_top = placed_rows(tops, (0, 160), x, (0, 1, 3))
    stream_low = placed_rows(lows, (0, 128), x, (0, 1, 3))
    def in_ring_order(v):
        v = v.reshape(4, 4, HD, -1).transpose(1, 0, 2, 3)
        v = lax.dynamic_slice_in_dim(jnp.concatenate([v, v], axis=0), x, 4, 0)
        n = v.shape[-1]
        parts = [v[:, :, :40].reshape(4, 160, n), v[:, :, 40:].reshape(4, 128, n)]
        return jnp.concatenate(parts, axis=1).reshape(D, n)

    weight = in_ring_order(w_sqkv).T.reshape(3, HD, D)
    weight = jnp.pad(weight, ((0, 0), (0, PAD - HD), (0, 0))).reshape(3 * PAD, D)
    shift_scale = in_ring_order(modulation[:2].T).T
    shift_scale = jnp.concatenate([shift_scale, jnp.zeros((6, D), F32)], axis=0)
    pieces, late, weight, shift_scale, modulation, stream_top, stream_low = together(
        (pieces, late, weight, shift_scale, modulation, stream_top, stream_low)
    )

    so_half = lax.all_gather(
        late[:, 2 * D :], "tensor", axis=0, tiled=True, axis_index_groups=x_groups
    )
    attended = spatial_attention(pieces, weight, shift_scale)
    stream_top = placed_rows(tops, (0, 160), x, (2,), stream_top)
    stream_low = placed_rows(lows, (0, 128), x, (2,), stream_low)
    stream = jnp.concatenate(
        [stream_top.reshape(4, 4, 40, ROWS), stream_low.reshape(4, 4, 32, ROWS)], axis=2
    )
    stream = row_major(stream.transpose(1, 0, 2, 3).reshape(D, ROWS).T)
    attended, late = together((attended, late))
    fc_all = lax.all_gather(
        late[:, : 2 * D], "tensor", axis=0, tiled=True, axis_index_groups=x_groups
    )
    attended = lax.all_to_all(attended, "tensor", split_axis=1, concat_axis=0, tiled=True)
    attended, head_a = together((attended, head_a))
    attended = attended.reshape(4, 4, HD, ROWS).transpose(1, 0, 2, 3).reshape(D, ROWS)
    attended = jnp.concatenate([attended, move_frame(attended, dcore=1)], axis=1)
    mine = dot(attended, so_half, ((0,), (0,))).astype(BF16)
    theirs = move_frame(mine[ROWS:], dcore=1)
    mine = mine[:ROWS]
    projected = jnp.where(
        core == 0, jnp.concatenate([mine, theirs], axis=1), jnp.concatenate([theirs, mine], axis=1)
    ).astype(F32)
    stream = row_major((stream.astype(F32) + modulation[2] * projected).astype(BF16))

    rows = jnp.concatenate([branch_input(stream, modulation[3], modulation[4]), table], axis=0)
    head_b = move_frame(head_a, dzl=1)
    column, head_b = together((gather_column(rows, y), head_b))
    rows = row_major(jnp.concatenate([column, move_frame(column, dcore=1)], axis=0))
    qkv_b = move_frame(rotated_qkv(rows, head_b[: 3 * HD]), dzl=1)
    qkv_a = rotated_qkv(rows, head_a[: 3 * HD])
    out_a, out_b = temporal_attention(qkv_a, qkv_b)
    out_b = move_frame(out_b, dzl=1)
    out = jnp.concatenate([out_a, out_b], axis=1)
    w_out = jnp.concatenate([head_a[3 * HD :], head_b[3 * HD :]], axis=0)
    partial = row_major(dot(out, w_out).astype(BF16))
    partial, fc_all = together((partial, fc_all))
    stream = row_major((stream.astype(F32) + modulation[5] * scatter_rows(partial)[:ROWS]).astype(BF16))

    rows = branch_input(stream, modulation[6], modulation[7])
    rows = jnp.concatenate([rows, move_frame(rows, dzl=1)], axis=0)
    rows = jnp.concatenate([rows, move_frame(rows, dcore=1)], axis=0)
    partial = mlp(rows, fc_all)
    partial = partial[: 2 * ROWS].astype(F32) + move_frame(partial[2 * ROWS :], dcore=1).astype(F32)
    partial = partial[:ROWS] + move_frame(partial[ROWS:].astype(BF16), dzl=1).astype(F32)
    stream = stream.astype(F32) + modulation[8] * partial
    return lax.all_to_all(stream.astype(BF16), "tensor", split_axis=1, concat_axis=0, tiled=True)


def solution(mesh):
    placed = (
        P("frame", "tensor"),
        P(),
        P("frame"),
        P(),
        P(None, "tensor"),
        P("tensor", None),
        P(None, "tensor"),
        P("tensor", None),
        P(None, "tensor"),
        P("tensor", None),
        P(None, "tensor"),
        P("tensor", None),
    )
    return jax.shard_map(
        shards, mesh=mesh, in_specs=placed, out_specs=P("frame", "tensor"), check_vma=False
    )
```

```python
import math

import jax
import jax.numpy as jnp
from jax import lax
from jax.experimental import pallas as pl
from jax.experimental.layout import Layout, with_layout_constraint
from jax.experimental.pallas import tpu as pltpu
from jax.sharding import PartitionSpec as P

D = 1152
HD = 72
P_SIZE = 1920
N_T = 16
ROWS = P_SIZE // N_T
FF_PART = 72
SCALE_LOG2 = HD ** (-0.5) * math.log2(math.e)
Q_BLOCK = 384
PAD = 80
BLOCK = 128
F32 = jnp.float32
BF16 = jnp.bfloat16


def layer_norm(values_in):
    center = values_in - jnp.mean(values_in, axis=-1, keepdims=True)
    spread = jnp.mean(center * center, axis=-1, keepdims=True)
    return center * lax.rsqrt(spread + 1e-06)


def branch_input(stream, shift, scale):
    return (layer_norm(stream.astype(F32)) * (1.0 + scale) + shift).astype(BF16)


def time_features(timestep, width):
    half_width = width // 2
    frequency = jnp.exp(-math.log(10000.0) * jnp.arange(half_width, dtype=F32) / half_width)
    angles = timestep.astype(F32)[:, None] * frequency[None, :]
    return jnp.concatenate([jnp.cos(angles), jnp.sin(angles)], axis=1).astype(BF16)


def dot(a, b, contract=((1,), (0,))):
    return lax.dot_general(a, b, (contract, ((), ())), preferred_element_type=F32)


def row_major(v):
    return with_layout_constraint(v, Layout(major_to_minor=tuple(range(v.ndim))))


def move_frame(v, dzl=0, dy=0, dcore=0):
    pairs = []
    for source in range(16):
        zl, y, core = source // 8, source // 2 % 4, source % 2
        pairs.append((source, (zl ^ dzl) * 8 + (y + dy) % 4 * 2 + (core ^ dcore)))
    return lax.ppermute(v, "frame", pairs)


def move_tensor(v, dzh=0, dx=0):
    pairs = []
    for source in range(16):
        zh, x = source // 4, source % 4
        pairs.append((source, (zh + dzh) % 4 * 4 + (x + dx) % 4))
    return lax.ppermute(v, "tensor", pairs)


def ring(own, move, half):
    return ring_far(own, move(own, 1), move(own, -1), move, half)


def ring_far(own, before, after, move, half):
    return own, after, move(before[:half], 1), move(after[half:], -1), before


def ring_in_halves(top, low, move):
    before_top, after_low = move(top, 1), move(low, -1)
    before_low, after_top = move(low, 1), move(top, -1)
    far_top, far_low = move(before_top, 1), move(after_low, -1)
    return (top, low), (after_top, after_low), (far_top, far_low), (before_top, before_low)


def placed_rows(blocks, rows, position, steps=(0, 1, 2, 3), out=None):
    if out is None:
        out = jnp.zeros((4, rows[1] - rows[0]) + blocks[0][0].shape[1:], blocks[0][0].dtype)
    for step in steps:
        parts = blocks[step]
        start = 0
        for part in parts:
            stop = start + part.shape[0]
            low, high = max(start, rows[0]), min(stop, rows[1])
            if low < high:
                piece = part[low - start : high - start][None]
                out = lax.dynamic_update_slice(out, piece, ((position + step) % 4, low - rows[0], 0))
            start = stop
    return out


def along_zh(v, d):
    return move_tensor(v, dzh=d)


def along_x(v, d):
    return move_tensor(v, dx=d)


def along_y(v, d):
    return move_frame(v, dy=d)


def gather_column(own, y):
    own, after, far_a, far_b, before = ring(row_major(own), along_y, 64)
    column = placed_rows(((own,), (after,), (far_a, far_b), (before,)), (0, BLOCK), y)
    return row_major(column.reshape(4 * BLOCK, D))


def scatter_rows(partial):
    n = partial.shape[0] // 2
    column = partial[:n].astype(F32) + move_frame(partial[n:], dcore=1).astype(F32)
    blocks = column.astype(BF16).reshape(4, n // 4, partial.shape[1])
    groups = [[8 * zl + 2 * y + core for y in range(4)] for zl in range(2) for core in range(2)]
    terms = lax.all_to_all(blocks, "frame", 0, 0, axis_index_groups=groups)
    return jnp.sum(terms.astype(F32), axis=0)


def spatial_kernel(*refs):
    pieces, (weight_ref, shift_scale_ref, out_ref, queries, keys, values) = refs[:8], refs[8:]

    shift_scale = shift_scale_ref[...].T
    shift, scale = shift_scale[:, 0:1], 1.0 + shift_scale[:, 1:2]
    ones_row = lax.broadcasted_iota(jnp.int32, (PAD, Q_BLOCK), 0) == HD
    parts = [slice(start, start + Q_BLOCK) for start in range(0, P_SIZE, Q_BLOCK)]
    for part in parts:
        rows = [ref[:, part] for ref in pieces]
        features = jnp.concatenate(rows, axis=0).astype(F32)
        center = features - jnp.mean(features, axis=0, keepdims=True)
        spread = jnp.mean(center * center, axis=0, keepdims=True)
        normed = center * lax.rsqrt(spread + 1e-06) * scale + shift
        qkv = dot(weight_ref[...], normed.astype(BF16))
        queries[:, part] = qkv[:PAD].astype(BF16)
        keys[part, :] = qkv[PAD : 2 * PAD].T.astype(BF16)
        values[:, part] = jnp.where(ones_row, 1.0, qkv[2 * PAD :]).astype(BF16)

    top = total = None
    for part in parts:
        scores = dot(keys[part, :], queries[...])
        block_top = jnp.max(scores, axis=0, keepdims=True) * SCALE_LOG2
        new_top = block_top if top is None else jnp.maximum(top, block_top)
        weights = jnp.exp2(scores * SCALE_LOG2 - new_top).astype(BF16)
        term = dot(values[:, part], weights)
        total = term if top is None else total * jnp.exp2(top - new_top) + term
        top = new_top
    out_ref[...] = (total[:HD] / total[HD : HD + 1]).astype(BF16)


def spatial_attention(pieces, weight, shift_scale):
    operands = (*pieces, weight, shift_scale)
    return pl.pallas_call(
        spatial_kernel,
        out_shape=jax.ShapeDtypeStruct((HD, P_SIZE), BF16),
        scratch_shapes=[
            pltpu.VMEM((PAD, P_SIZE), BF16),
            pltpu.VMEM((P_SIZE, PAD), BF16),
            pltpu.VMEM((PAD, P_SIZE), BF16),
        ],
        compiler_params=pltpu.CompilerParams(vmem_limit_bytes=48 * 2**20),
        cost_estimate=pl.CostEstimate(
            flops=4 * P_SIZE * P_SIZE * HD + 2 * P_SIZE * D * 3 * HD,
            bytes_accessed=P_SIZE * D * 2,
            transcendentals=P_SIZE * P_SIZE,
        ),
    )(*operands)


def mlp_kernel(rows_ref, weight_ref, out_ref):
    total = jnp.zeros(out_ref.shape, F32)
    step = 384
    for start in range(0, D, step):
        units = slice(start, start + step)
        hidden = dot(rows_ref[...], weight_ref[units, :D], ((1,), (1,)))
        hidden = jax.nn.gelu(hidden, approximate=True).astype(BF16)
        total = total + dot(hidden, weight_ref[units, D:])
    out_ref[...] = total.astype(BF16)


def mlp(rows, weight):
    return pl.pallas_call(
        mlp_kernel,
        out_shape=jax.ShapeDtypeStruct(rows.shape, BF16),
        compiler_params=pltpu.CompilerParams(vmem_limit_bytes=40 * 2**20),
        cost_estimate=pl.CostEstimate(
            flops=4 * rows.shape[0] * D * D, bytes_accessed=6 * D * D, transcendentals=rows.shape[0] * D
        ),
    )(rows, weight)


def rotated_kernel(rows_ref, weight_ref, swap_ref, out_ref):
    projected = dot(rows_ref[...], weight_ref[...], ((1,), (1,))).astype(BF16)
    swapped = dot(projected, swap_ref[...])
    projected = projected.astype(F32)
    for frame in range(8):
        rows = slice(BLOCK * frame, BLOCK * frame + BLOCK)
        table = rows_ref[BLOCK * frame + BLOCK - 16 : BLOCK * frame + BLOCK, : 3 * HD].astype(F32)
        cosine, sine = table[8:9] + table[9:10], table[10:11] + table[11:12]
        out_ref[rows] = (projected[rows] * cosine + swapped[rows] * sine).astype(BF16)


def rotated_qkv(rows, weight):
    lane = jnp.arange(3 * HD)
    half = HD // 2
    partner = jnp.where(lane % HD < half, lane + half, lane - half)
    swap = ((lane[:, None] == partner[None, :]) & (lane[None, :] < 2 * HD)).astype(BF16)
    return pl.pallas_call(
        rotated_kernel,
        out_shape=jax.ShapeDtypeStruct((8 * BLOCK, 3 * HD), BF16),
        compiler_params=pltpu.CompilerParams(vmem_limit_bytes=32 * 2**20),
        cost_estimate=pl.CostEstimate(
            flops=16 * BLOCK * D * 3 * HD, bytes_accessed=16 * BLOCK * D, transcendentals=0
        ),
    )(rows, weight, swap)


def rotation_table(position):
    half = HD // 2
    frequency = jnp.exp(-math.log(10000.0) * jnp.arange(half, dtype=F32) / half)
    angles = position.astype(F32) * frequency
    cosine, sine = jnp.cos(angles), jnp.sin(angles)
    cosine = jnp.concatenate([cosine] * 4 + [jnp.ones((HD,), F32)])
    sine = jnp.concatenate([-sine, sine] * 2 + [jnp.zeros((HD,), F32)])
    rows = []
    for values in (cosine, sine):
        high = lax.reduce_precision(values, 8, 7)
        rows += [high.astype(BF16), (values - high).astype(BF16)]
    return jnp.pad(jnp.stack(rows), ((0, 4), (0, D - 3 * HD)))


def temporal_kernel(own_ref, other_ref, out_own_ref, out_other_ref):
    row = lax.broadcasted_iota(jnp.int32, (256, 256), 0)
    column = lax.broadcasted_iota(jnp.int32, (256, 256), 1)
    same = (row % 16) == (column % 16)
    for group in range(BLOCK // 16):
        rows = [slice(BLOCK * frame + 16 * group, BLOCK * frame + 16 * group + 16) for frame in range(8)]
        section = jnp.concatenate([ref[r, :] for ref in (own_ref, other_ref) for r in rows], axis=0)
        queries, keys, values = section[:, :HD], section[:, HD : 2 * HD], section[:, 2 * HD :]
        scores = jnp.where(same, dot(queries, keys, ((1,), (1,))), -jnp.inf)
        top = jnp.max(scores, axis=1, keepdims=True)
        weights = jnp.exp2((scores - top) * SCALE_LOG2)
        weights = (weights / jnp.sum(weights, axis=1, keepdims=True)).astype(BF16)
        result = dot(weights, values).astype(BF16)
        for index, r in enumerate(rows):
            out_own_ref[r, :] = result[16 * index : 16 * index + 16]
            out_other_ref[r, :] = result[128 + 16 * index : 144 + 16 * index]


def temporal_attention(own, other):
    shape = jax.ShapeDtypeStruct((8 * BLOCK, HD), BF16)
    return pl.pallas_call(
        temporal_kernel,
        out_shape=(shape, shape),
        compiler_params=pltpu.CompilerParams(vmem_limit_bytes=32 * 2**20),
        cost_estimate=pl.CostEstimate(
            flops=16 * BLOCK * 256 * HD * 4, bytes_accessed=16 * BLOCK * HD * 8, transcendentals=16 * BLOCK * 256
        ),
    )(own, other)


def shards(
    latent, timestep, frame_pos, time_w1, time_w2, ada_w, w_sqkv, w_so, w_tqkv, w_to, w_fc1, w_fc2
):
    frame = lax.axis_index("frame")
    tensor = lax.axis_index("tensor")
    zl, y, core = frame // 8, frame // 2 % 4, frame % 2

    zh, x = tensor // 4, tensor % 4
    together = lax.optimization_barrier

    zh_groups = [[4 * i + j for i in range(4)] for j in range(4)]
    x_groups = [[4 * i + j for j in range(4)] for i in range(4)]

    pairs = []
    for f in range(16):
        turn = f % 2 * 2 + f // 8
        for t in range(16):
            head = (t // 4 + turn) % 4 * 4 + (t + f // 2 % 4 + turn) % 4
            pairs.append((f * 16 + head, f * 16 + t))
    head_a = lax.ppermute(jnp.concatenate([w_tqkv.T, w_to], axis=0), ("frame", "tensor"), pairs)

    own = latent.T
    before, after, w_fc1, w_fc2, w_so = together(
        (along_zh(own, 1), along_zh(own, -1), w_fc1, w_fc2, w_so)
    )
    own, after, far_top, far_low, before = ring_far(own, before, after, along_zh, 40)
    blocks = (own,), (after,), (far_top, far_low), (before,)
    latent_top = placed_rows(blocks, (0, 40), zh).reshape(160, P_SIZE)
    latent_low = placed_rows(blocks, (40, HD), zh).reshape(128, P_SIZE)

    part = (zl * 2 + core) * FF_PART
    late = jnp.concatenate(
        [
            lax.dynamic_slice_in_dim(w_fc1, part, FF_PART, 1).T,
            lax.dynamic_slice_in_dim(w_fc2, part, FF_PART, 0),
            lax.dynamic_slice_in_dim(w_so, core * (D // 2), D // 2, 1),
        ],
        axis=1,
    )

    time_embed = time_features(timestep, time_w1.shape[0])
    hidden_time = jax.nn.silu(dot(time_embed, time_w1)).astype(BF16)
    condition = jax.nn.silu(dot(hidden_time, time_w2)).astype(BF16)
    terms = dot(condition, ada_w).astype(BF16).reshape(1, 9, D)
    table = rotation_table(frame_pos)
    latent_top, latent_low, w_sqkv, terms, table, head_a = together(
        (latent_top, latent_low, w_sqkv, terms, table, head_a)
    )
    terms = lax.all_to_all(jnp.broadcast_to(terms, (N_T, 9, D)), "tensor", 0, 0)
    late = lax.all_gather(late, "tensor", axis=0, tiled=True, axis_index_groups=zh_groups)
    blocks = ring_in_halves(latent_top, latent_low, along_x)
    modulation = jnp.sum(terms.astype(F32), axis=0)
    pieces = [part for block in blocks for part in block]
    stream = [[lax.dynamic_slice_in_dim(p, tensor * ROWS, ROWS, 1) for p in block] for block in blocks]
    tops, lows = [(block[0],) for block in stream], [(block[1],) for block in stream]
    stream_top = placed_rows(tops, (0, 160), x, (0, 1, 3))
    stream_low = placed_rows(lows, (0, 128), x, (0, 1, 3))
    def in_ring_order(v):
        v = v.reshape(4, 4, HD, -1).transpose(1, 0, 2, 3)
        v = lax.dynamic_slice_in_dim(jnp.concatenate([v, v], axis=0), x, 4, 0)
        n = v.shape[-1]
        parts = [v[:, :, :40].reshape(4, 160, n), v[:, :, 40:].reshape(4, 128, n)]
        return jnp.concatenate(parts, axis=1).reshape(D, n)

    weight = in_ring_order(w_sqkv).T.reshape(3, HD, D)
    weight = jnp.pad(weight, ((0, 0), (0, PAD - HD), (0, 0))).reshape(3 * PAD, D)
    shift_scale = in_ring_order(modulation[:2].T).T
    shift_scale = jnp.concatenate([shift_scale, jnp.zeros((6, D), F32)], axis=0)
    pieces, late, weight, shift_scale, modulation, stream_top, stream_low = together(
        (pieces, late, weight, shift_scale, modulation, stream_top, stream_low)
    )

    so_half = lax.all_gather(
        late[:, 2 * D :], "tensor", axis=0, tiled=True, axis_index_groups=x_groups
    )
    attended = spatial_attention(pieces, weight, shift_scale)
    stream_top = placed_rows(tops, (0, 160), x, (2,), stream_top)
    stream_low = placed_rows(lows, (0, 128), x, (2,), stream_low)
    stream = jnp.concatenate(
        [stream_top.reshape(4, 4, 40, ROWS), stream_low.reshape(4, 4, 32, ROWS)], axis=2
    )
    stream = row_major(stream.transpose(1, 0, 2, 3).reshape(D, ROWS).T)
    attended, late = together((attended, late))
    fc_all = lax.all_gather(
        late[:, : 2 * D], "tensor", axis=0, tiled=True, axis_index_groups=x_groups
    )
    attended = lax.all_to_all(attended, "tensor", split_axis=1, concat_axis=0, tiled=True)
    attended, head_a = together((attended, head_a))
    attended = attended.reshape(4, 4, HD, ROWS).transpose(1, 0, 2, 3).reshape(D, ROWS)
    attended = jnp.concatenate([attended, move_frame(attended, dcore=1)], axis=1)
    mine = dot(attended, so_half, ((0,), (0,))).astype(BF16)
    theirs = move_frame(mine[ROWS:], dcore=1)
    mine = mine[:ROWS]
    projected = jnp.where(
        core == 0, jnp.concatenate([mine, theirs], axis=1), jnp.concatenate([theirs, mine], axis=1)
    ).astype(F32)
    stream = row_major((stream.astype(F32) + modulation[2] * projected).astype(BF16))

    rows = jnp.concatenate([branch_input(stream, modulation[3], modulation[4]), table], axis=0)
    head_b = move_frame(head_a, dzl=1)
    column, head_b = together((gather_column(rows, y), head_b))
    rows = row_major(jnp.concatenate([column, move_frame(column, dcore=1)], axis=0))
    qkv_b = move_frame(rotated_qkv(rows, head_b[: 3 * HD]), dzl=1)
    qkv_a = rotated_qkv(rows, head_a[: 3 * HD])
    out_a, out_b = temporal_attention(qkv_a, qkv_b)
    out_b = move_frame(out_b, dzl=1)
    out = jnp.concatenate([out_a, out_b], axis=1)
    w_out = jnp.concatenate([head_a[3 * HD :], head_b[3 * HD :]], axis=0)
    partial = dot(out, w_out).astype(BF16)
    stream = row_major((stream.astype(F32) + modulation[5] * scatter_rows(partial)[:ROWS]).astype(BF16))
    stream, fc_all = together((stream, fc_all))

    rows = branch_input(stream, modulation[6], modulation[7])
    rows = jnp.concatenate([rows, move_frame(rows, dzl=1)], axis=0)
    rows = jnp.concatenate([rows, move_frame(rows, dcore=1)], axis=0)
    partial = mlp(rows, fc_all)
    partial = partial[: 2 * ROWS].astype(F32) + move_frame(partial[2 * ROWS :], dcore=1).astype(F32)
    partial = partial[:ROWS] + move_frame(partial[ROWS:].astype(BF16), dzl=1).astype(F32)
    stream = stream.astype(F32) + modulation[8] * partial
    return lax.all_to_all(stream.astype(BF16), "tensor", split_axis=1, concat_axis=0, tiled=True)


def solution(mesh):
    placed = (
        P("frame", "tensor"),
        P(),
        P("frame"),
        P(),
        P(None, "tensor"),
        P("tensor", None),
        P(None, "tensor"),
        P("tensor", None),
        P(None, "tensor"),
        P("tensor", None),
        P(None, "tensor"),
        P("tensor", None),
    )
    return jax.shard_map(
        shards, mesh=mesh, in_specs=placed, out_specs=P("frame", "tensor"), check_vma=False
    )
```

```python
import math

import jax
import jax.numpy as jnp
from jax import lax
from jax.experimental import pallas as pl
from jax.experimental.layout import Layout, with_layout_constraint
from jax.experimental.pallas import tpu as pltpu
from jax.sharding import PartitionSpec as P

D = 1152
HD = 72
P_SIZE = 1920
N_T = 16
ROWS = P_SIZE // N_T
FF_PART = 72
SCALE_LOG2 = HD ** (-0.5) * math.log2(math.e)
Q_BLOCK = 384
PAD = 80
BLOCK = 128
F32 = jnp.float32
BF16 = jnp.bfloat16


def layer_norm(values_in):
    center = values_in - jnp.mean(values_in, axis=-1, keepdims=True)
    spread = jnp.mean(center * center, axis=-1, keepdims=True)
    return center * lax.rsqrt(spread + 1e-06)


def branch_input(stream, shift, scale):
    return (layer_norm(stream.astype(F32)) * (1.0 + scale) + shift).astype(BF16)


def time_features(timestep, width):
    half_width = width // 2
    frequency = jnp.exp(-math.log(10000.0) * jnp.arange(half_width, dtype=F32) / half_width)
    angles = timestep.astype(F32)[:, None] * frequency[None, :]
    return jnp.concatenate([jnp.cos(angles), jnp.sin(angles)], axis=1).astype(BF16)


def dot(a, b, contract=((1,), (0,))):
    return lax.dot_general(a, b, (contract, ((), ())), preferred_element_type=F32)


def row_major(v):
    return with_layout_constraint(v, Layout(major_to_minor=tuple(range(v.ndim))))


def move_frame(v, dzl=0, dy=0, dcore=0):
    pairs = []
    for source in range(16):
        zl, y, core = source // 8, source // 2 % 4, source % 2
        pairs.append((source, (zl ^ dzl) * 8 + (y + dy) % 4 * 2 + (core ^ dcore)))
    return lax.ppermute(v, "frame", pairs)


def move_tensor(v, dzh=0, dx=0):
    pairs = []
    for source in range(16):
        zh, x = source // 4, source % 4
        pairs.append((source, (zh + dzh) % 4 * 4 + (x + dx) % 4))
    return lax.ppermute(v, "tensor", pairs)


def ring(own, move, half):
    return ring_far(own, move(own, 1), move(own, -1), move, half)


def ring_far(own, before, after, move, half):
    return own, after, move(before[:half], 1), move(after[half:], -1), before


def ring_in_halves(top, low, move):
    before_top, after_low = move(top, 1), move(low, -1)
    before_low, after_top = move(low, 1), move(top, -1)
    far_top, far_low = move(before_top, 1), move(after_low, -1)
    return (top, low), (after_top, after_low), (far_top, far_low), (before_top, before_low)


def placed_rows(blocks, rows, position, steps=(0, 1, 2, 3), out=None):
    if out is None:
        out = jnp.zeros((4, rows[1] - rows[0]) + blocks[0][0].shape[1:], blocks[0][0].dtype)
    for step in steps:
        parts = blocks[step]
        start = 0
        for part in parts:
            stop = start + part.shape[0]
            low, high = max(start, rows[0]), min(stop, rows[1])
            if low < high:
                piece = part[low - start : high - start][None]
                out = lax.dynamic_update_slice(out, piece, ((position + step) % 4, low - rows[0], 0))
            start = stop
    return out


def along_zh(v, d):
    return move_tensor(v, dzh=d)


def along_x(v, d):
    return move_tensor(v, dx=d)


def along_y(v, d):
    return move_frame(v, dy=d)


def gather_column(own, y):
    own, after, far_a, far_b, before = ring(row_major(own), along_y, 64)
    column = placed_rows(((own,), (after,), (far_a, far_b), (before,)), (0, BLOCK), y)
    return row_major(column.reshape(4 * BLOCK, D))


def scatter_rows(partial, weight):
    n = partial.shape[0] // 2
    column = partial[:n].astype(F32) + move_frame(partial[n:], dcore=1).astype(F32)
    column, weight = lax.optimization_barrier((column.astype(BF16), weight))
    blocks = column.reshape(4, n // 4, partial.shape[1])
    groups = [[8 * zl + 2 * y + core for y in range(4)] for zl in range(2) for core in range(2)]
    terms = lax.all_to_all(blocks, "frame", 0, 0, axis_index_groups=groups)
    return jnp.sum(terms.astype(F32), axis=0), weight


def spatial_kernel(*refs):
    pieces, (weight_ref, shift_scale_ref, out_ref, queries, keys, values) = refs[:8], refs[8:]

    shift_scale = shift_scale_ref[...].T
    shift, scale = shift_scale[:, 0:1], 1.0 + shift_scale[:, 1:2]
    ones_row = lax.broadcasted_iota(jnp.int32, (PAD, Q_BLOCK), 0) == HD
    parts = [slice(start, start + Q_BLOCK) for start in range(0, P_SIZE, Q_BLOCK)]
    for part in parts:
        rows = [ref[:, part] for ref in pieces]
        features = jnp.concatenate(rows, axis=0).astype(F32)
        center = features - jnp.mean(features, axis=0, keepdims=True)
        spread = jnp.mean(center * center, axis=0, keepdims=True)
        normed = center * lax.rsqrt(spread + 1e-06) * scale + shift
        qkv = dot(weight_ref[...], normed.astype(BF16))
        queries[:, part] = qkv[:PAD].astype(BF16)
        keys[part, :] = qkv[PAD : 2 * PAD].T.astype(BF16)
        values[:, part] = jnp.where(ones_row, 1.0, qkv[2 * PAD :]).astype(BF16)

    top = total = None
    for part in parts:
        scores = dot(keys[part, :], queries[...])
        block_top = jnp.max(scores, axis=0, keepdims=True) * SCALE_LOG2
        new_top = block_top if top is None else jnp.maximum(top, block_top)
        weights = jnp.exp2(scores * SCALE_LOG2 - new_top).astype(BF16)
        term = dot(values[:, part], weights)
        total = term if top is None else total * jnp.exp2(top - new_top) + term
        top = new_top
    out_ref[...] = (total[:HD] / total[HD : HD + 1]).astype(BF16)


def spatial_attention(pieces, weight, shift_scale):
    operands = (*pieces, weight, shift_scale)
    return pl.pallas_call(
        spatial_kernel,
        out_shape=jax.ShapeDtypeStruct((HD, P_SIZE), BF16),
        scratch_shapes=[
            pltpu.VMEM((PAD, P_SIZE), BF16),
            pltpu.VMEM((P_SIZE, PAD), BF16),
            pltpu.VMEM((PAD, P_SIZE), BF16),
        ],
        compiler_params=pltpu.CompilerParams(vmem_limit_bytes=48 * 2**20),
        cost_estimate=pl.CostEstimate(
            flops=4 * P_SIZE * P_SIZE * HD + 2 * P_SIZE * D * 3 * HD,
            bytes_accessed=P_SIZE * D * 2,
            transcendentals=P_SIZE * P_SIZE,
        ),
    )(*operands)


def mlp_kernel(rows_ref, weight_ref, out_ref):
    total = jnp.zeros(out_ref.shape, F32)
    step = 384
    for start in range(0, D, step):
        units = slice(start, start + step)
        hidden = dot(rows_ref[...], weight_ref[units, :D], ((1,), (1,)))
        hidden = jax.nn.gelu(hidden, approximate=True).astype(BF16)
        total = total + dot(hidden, weight_ref[units, D:])
    out_ref[...] = total.astype(BF16)


def mlp(rows, weight):
    return pl.pallas_call(
        mlp_kernel,
        out_shape=jax.ShapeDtypeStruct(rows.shape, BF16),
        compiler_params=pltpu.CompilerParams(vmem_limit_bytes=40 * 2**20),
        cost_estimate=pl.CostEstimate(
            flops=4 * rows.shape[0] * D * D, bytes_accessed=6 * D * D, transcendentals=rows.shape[0] * D
        ),
    )(rows, weight)


def rotated_kernel(rows_ref, weight_ref, swap_ref, out_ref):
    projected = dot(rows_ref[...], weight_ref[...], ((1,), (1,))).astype(BF16)
    swapped = dot(projected, swap_ref[...])
    projected = projected.astype(F32)
    for frame in range(8):
        rows = slice(BLOCK * frame, BLOCK * frame + BLOCK)
        table = rows_ref[BLOCK * frame + BLOCK - 16 : BLOCK * frame + BLOCK, : 3 * HD].astype(F32)
        cosine, sine = table[8:9] + table[9:10], table[10:11] + table[11:12]
        out_ref[rows] = (projected[rows] * cosine + swapped[rows] * sine).astype(BF16)


def rotated_qkv(rows, weight):
    lane = jnp.arange(3 * HD)
    half = HD // 2
    partner = jnp.where(lane % HD < half, lane + half, lane - half)
    swap = ((lane[:, None] == partner[None, :]) & (lane[None, :] < 2 * HD)).astype(BF16)
    return pl.pallas_call(
        rotated_kernel,
        out_shape=jax.ShapeDtypeStruct((8 * BLOCK, 3 * HD), BF16),
        compiler_params=pltpu.CompilerParams(vmem_limit_bytes=32 * 2**20),
        cost_estimate=pl.CostEstimate(
            flops=16 * BLOCK * D * 3 * HD, bytes_accessed=16 * BLOCK * D, transcendentals=0
        ),
    )(rows, weight, swap)


def rotation_table(position):
    half = HD // 2
    frequency = jnp.exp(-math.log(10000.0) * jnp.arange(half, dtype=F32) / half)
    angles = position.astype(F32) * frequency
    cosine, sine = jnp.cos(angles), jnp.sin(angles)
    cosine = jnp.concatenate([cosine] * 4 + [jnp.ones((HD,), F32)])
    sine = jnp.concatenate([-sine, sine] * 2 + [jnp.zeros((HD,), F32)])
    rows = []
    for values in (cosine, sine):
        high = lax.reduce_precision(values, 8, 7)
        rows += [high.astype(BF16), (values - high).astype(BF16)]
    return jnp.pad(jnp.stack(rows), ((0, 4), (0, D - 3 * HD)))


def temporal_kernel(own_ref, other_ref, out_own_ref, out_other_ref):
    row = lax.broadcasted_iota(jnp.int32, (256, 256), 0)
    column = lax.broadcasted_iota(jnp.int32, (256, 256), 1)
    same = (row % 16) == (column % 16)
    for group in range(BLOCK // 16):
        rows = [slice(BLOCK * frame + 16 * group, BLOCK * frame + 16 * group + 16) for frame in range(8)]
        section = jnp.concatenate([ref[r, :] for ref in (own_ref, other_ref) for r in rows], axis=0)
        queries, keys, values = section[:, :HD], section[:, HD : 2 * HD], section[:, 2 * HD :]
        scores = jnp.where(same, dot(queries, keys, ((1,), (1,))), -jnp.inf)
        top = jnp.max(scores, axis=1, keepdims=True)
        weights = jnp.exp2((scores - top) * SCALE_LOG2)
        weights = (weights / jnp.sum(weights, axis=1, keepdims=True)).astype(BF16)
        result = dot(weights, values).astype(BF16)
        for index, r in enumerate(rows):
            out_own_ref[r, :] = result[16 * index : 16 * index + 16]
            out_other_ref[r, :] = result[128 + 16 * index : 144 + 16 * index]


def temporal_attention(own, other):
    shape = jax.ShapeDtypeStruct((8 * BLOCK, HD), BF16)
    return pl.pallas_call(
        temporal_kernel,
        out_shape=(shape, shape),
        compiler_params=pltpu.CompilerParams(vmem_limit_bytes=32 * 2**20),
        cost_estimate=pl.CostEstimate(
            flops=16 * BLOCK * 256 * HD * 4, bytes_accessed=16 * BLOCK * HD * 8, transcendentals=16 * BLOCK * 256
        ),
    )(own, other)


def shards(
    latent, timestep, frame_pos, time_w1, time_w2, ada_w, w_sqkv, w_so, w_tqkv, w_to, w_fc1, w_fc2
):
    frame = lax.axis_index("frame")
    tensor = lax.axis_index("tensor")
    zl, y, core = frame // 8, frame // 2 % 4, frame % 2

    zh, x = tensor // 4, tensor % 4
    together = lax.optimization_barrier

    zh_groups = [[4 * i + j for i in range(4)] for j in range(4)]
    x_groups = [[4 * i + j for j in range(4)] for i in range(4)]

    pairs = []
    for f in range(16):
        turn = f % 2 * 2 + f // 8
        for t in range(16):
            head = (t // 4 + turn) % 4 * 4 + (t + f // 2 % 4 + turn) % 4
            pairs.append((f * 16 + head, f * 16 + t))
    head_a = lax.ppermute(jnp.concatenate([w_tqkv.T, w_to], axis=0), ("frame", "tensor"), pairs)

    own = latent.T
    before, after, w_fc1, w_fc2, w_so = together(
        (along_zh(own, 1), along_zh(own, -1), w_fc1, w_fc2, w_so)
    )
    own, after, far_top, far_low, before = ring_far(own, before, after, along_zh, 40)
    blocks = (own,), (after,), (far_top, far_low), (before,)
    latent_top = placed_rows(blocks, (0, 40), zh).reshape(160, P_SIZE)
    latent_low = placed_rows(blocks, (40, HD), zh).reshape(128, P_SIZE)

    part = (zl * 2 + core) * FF_PART
    late = jnp.concatenate(
        [
            lax.dynamic_slice_in_dim(w_fc1, part, FF_PART, 1).T,
            lax.dynamic_slice_in_dim(w_fc2, part, FF_PART, 0),
            lax.dynamic_slice_in_dim(w_so, core * (D // 2), D // 2, 1),
        ],
        axis=1,
    )

    time_embed = time_features(timestep, time_w1.shape[0])
    hidden_time = jax.nn.silu(dot(time_embed, time_w1)).astype(BF16)
    condition = jax.nn.silu(dot(hidden_time, time_w2)).astype(BF16)
    terms = dot(condition, ada_w).astype(BF16).reshape(1, 9, D)
    table = rotation_table(frame_pos)
    latent_top, latent_low, w_sqkv, terms, table, head_a = together(
        (latent_top, latent_low, w_sqkv, terms, table, head_a)
    )
    terms = lax.all_to_all(jnp.broadcast_to(terms, (N_T, 9, D)), "tensor", 0, 0)
    late = lax.all_gather(late, "tensor", axis=0, tiled=True, axis_index_groups=zh_groups)
    blocks = ring_in_halves(latent_top, latent_low, along_x)
    modulation = jnp.sum(terms.astype(F32), axis=0)
    pieces = [part for block in blocks for part in block]
    stream = [[lax.dynamic_slice_in_dim(p, tensor * ROWS, ROWS, 1) for p in block] for block in blocks]
    tops, lows = [(block[0],) for block in stream], [(block[1],) for block in stream]
    stream_top = placed_rows(tops, (0, 160), x, (0, 1, 3))
    stream_low = placed_rows(lows, (0, 128), x, (0, 1, 3))
    def in_ring_order(v):
        v = v.reshape(4, 4, HD, -1).transpose(1, 0, 2, 3)
        v = lax.dynamic_slice_in_dim(jnp.concatenate([v, v], axis=0), x, 4, 0)
        n = v.shape[-1]
        parts = [v[:, :, :40].reshape(4, 160, n), v[:, :, 40:].reshape(4, 128, n)]
        return jnp.concatenate(parts, axis=1).reshape(D, n)

    weight = in_ring_order(w_sqkv).T.reshape(3, HD, D)
    weight = jnp.pad(weight, ((0, 0), (0, PAD - HD), (0, 0))).reshape(3 * PAD, D)
    shift_scale = in_ring_order(modulation[:2].T).T
    shift_scale = jnp.concatenate([shift_scale, jnp.zeros((6, D), F32)], axis=0)
    pieces, late, weight, shift_scale, modulation, stream_top, stream_low = together(
        (pieces, late, weight, shift_scale, modulation, stream_top, stream_low)
    )

    so_half = lax.all_gather(
        late[:, 2 * D :], "tensor", axis=0, tiled=True, axis_index_groups=x_groups
    )
    attended = spatial_attention(pieces, weight, shift_scale)
    stream_top = placed_rows(tops, (0, 160), x, (2,), stream_top)
    stream_low = placed_rows(lows, (0, 128), x, (2,), stream_low)
    stream = jnp.concatenate(
        [stream_top.reshape(4, 4, 40, ROWS), stream_low.reshape(4, 4, 32, ROWS)], axis=2
    )
    stream = row_major(stream.transpose(1, 0, 2, 3).reshape(D, ROWS).T)
    attended, late = together((attended, late))
    fc_all = lax.all_gather(
        late[:, : 2 * D], "tensor", axis=0, tiled=True, axis_index_groups=x_groups
    )
    attended = lax.all_to_all(attended, "tensor", split_axis=1, concat_axis=0, tiled=True)
    attended, head_a = together((attended, head_a))
    attended = attended.reshape(4, 4, HD, ROWS).transpose(1, 0, 2, 3).reshape(D, ROWS)
    attended = jnp.concatenate([attended, move_frame(attended, dcore=1)], axis=1)
    mine = dot(attended, so_half, ((0,), (0,))).astype(BF16)
    theirs = move_frame(mine[ROWS:], dcore=1)
    mine = mine[:ROWS]
    projected = jnp.where(
        core == 0, jnp.concatenate([mine, theirs], axis=1), jnp.concatenate([theirs, mine], axis=1)
    ).astype(F32)
    stream = row_major((stream.astype(F32) + modulation[2] * projected).astype(BF16))

    rows = jnp.concatenate([branch_input(stream, modulation[3], modulation[4]), table], axis=0)
    head_b = move_frame(head_a, dzl=1)
    column, head_b = together((gather_column(rows, y), head_b))
    rows = row_major(jnp.concatenate([column, move_frame(column, dcore=1)], axis=0))
    qkv_b = move_frame(rotated_qkv(rows, head_b[: 3 * HD]), dzl=1)
    qkv_a = rotated_qkv(rows, head_a[: 3 * HD])
    out_a, out_b = temporal_attention(qkv_a, qkv_b)
    out_b = move_frame(out_b, dzl=1)
    out = jnp.concatenate([out_a, out_b], axis=1)
    w_out = jnp.concatenate([head_a[3 * HD :], head_b[3 * HD :]], axis=0)
    partial = dot(out, w_out).astype(BF16)
    summed, fc_all = scatter_rows(partial, fc_all)
    stream = row_major((stream.astype(F32) + modulation[5] * summed[:ROWS]).astype(BF16))

    rows = branch_input(stream, modulation[6], modulation[7])
    rows = jnp.concatenate([rows, move_frame(rows, dzl=1)], axis=0)
    rows = jnp.concatenate([rows, move_frame(rows, dcore=1)], axis=0)
    partial = mlp(rows, fc_all)
    partial = partial[: 2 * ROWS].astype(F32) + move_frame(partial[2 * ROWS :], dcore=1).astype(F32)
    partial = partial[:ROWS] + move_frame(partial[ROWS:].astype(BF16), dzl=1).astype(F32)
    stream = stream.astype(F32) + modulation[8] * partial
    return lax.all_to_all(stream.astype(BF16), "tensor", split_axis=1, concat_axis=0, tiled=True)


def solution(mesh):
    placed = (
        P("frame", "tensor"),
        P(),
        P("frame"),
        P(),
        P(None, "tensor"),
        P("tensor", None),
        P(None, "tensor"),
        P("tensor", None),
        P(None, "tensor"),
        P("tensor", None),
        P(None, "tensor"),
        P("tensor", None),
    )
    return jax.shard_map(
        shards, mesh=mesh, in_specs=placed, out_specs=P("frame", "tensor"), check_vma=False
    )
```
